256 devices in a mesh: seq: 64 (over z, y_hi, x), head: 4 (over y_lo, core).
Axes of the slice: x: 4, y: 4 (y_hi: 2, y_lo: 2; y = y_hi * 2 + y_lo), z: 8, core: 2. Of those that a mesh axis runs over, the one named last changes fastest.
Arguments:
- q_shared: bfloat16 [8192, 512], P('seq'), may hold values from -4 to 4
- k_shared: bfloat16 [8192, 512], P('seq'), may hold values from -4 to 4
- mixing: float32 [64, 512], P('head'), may hold values from 0.25 to 2
- values: bfloat16 [8192, 8192], P('seq', 'head'), may hold values from -6 to 6
- cotangent: bfloat16 [8192, 8192], P('seq', 'head'), may hold values from -24 to 24
Outputs:
- d_query: bfloat16 [8192, 512], P('seq', 'head')
- d_key: bfloat16 [8192, 512], P('seq', 'head')
- d_values: bfloat16 [8192, 8192], P('seq', 'head')
- d_mixing: float32 [64, 512], P('head')
The draws below stay inside these ranges and needn't reach their ends.
All inputs are finite; a program needn't handle non-finite values.
Results may differ from the reference program's by a relative error of at most 0.011.
Values may be sent and summed in bfloat16 or wider, within the bound.
No kernel may reach another device: no remote copies, remote signals or barrier semaphores. Data moves between devices by JAX's collectives and lax.ppermute only.
A program may use at most 128 MiB of HBM per device.

```python
import math
import jax
import jax.numpy as jnp
from jax import lax

D_QK = 512
HEADS = 64
HEAD_DIM = 128
WINDOW = 512
TOK_DEV = 128
TOKENS = 8192


def draw_q_shared(key, part):
    key = jax.random.fold_in(key, 1)
    base = jax.random.truncated_normal(key, -4.0, 4.0, (TOKENS, D_QK), jnp.float32)
    return base.astype(jnp.bfloat16)


def draw_k_shared(key, part):
    key = jax.random.fold_in(key, 2)
    base = jax.random.truncated_normal(key, -4.0, 4.0, (TOKENS, D_QK), jnp.float32)
    return base.astype(jnp.bfloat16)


def steps_of(stream_key, dims, pieces, least, largest):
    def one(axis_at, shards_of):
        draws = jax.random.uniform(jax.random.fold_in(jax.random.fold_in(stream_key, 6), axis_at), (shards_of,), jnp.float32, least / len(pieces), largest / len(pieces))
        return jnp.repeat(jnp.exp(draws), dims[axis_at] // shards_of).reshape((-1,) + (1,) * (len(dims) - axis_at - 1))

    loudness = one(*pieces[0])
    for cut in pieces[1:]:
        loudness = loudness * one(*cut)
    return loudness


def normal_values(rng, dims, deviation, limit, pieces=(), held_as=jnp.bfloat16):
    factor_of = steps_of(rng, dims, pieces, -0.22, 0.18) if pieces else 1.0
    result = jax.random.normal(rng, dims, jnp.float32) * deviation * factor_of
    return jnp.minimum(jnp.maximum(result, -limit), limit).astype(held_as)


def setup_inputs(seed: int = 0) -> dict:
    seeds = jax.random.split(jax.random.key(seed), 6)
    return {
        "q_shared": draw_q_shared(jax.random.fold_in(seeds[5], 71), 0),
        "k_shared": draw_k_shared(jax.random.fold_in(seeds[5], 71), 0),
        "mixing": jnp.clip(jnp.exp(math.log(2.0) - 2.0794415 * jax.random.uniform(seeds[2], (HEADS, D_QK), jnp.float32) ** steps_of(seeds[2], (HEADS, D_QK), ((0, 4),), -0.2, 0.2)), 0.25, 2.0),
        "values": normal_values(seeds[3], (TOKENS, HEADS * HEAD_DIM), 1.0, 6.0, ((0, 64), (1, 4))),
        "cotangent": normal_values(seeds[4], (TOKENS, HEADS * HEAD_DIM), 4.0, 24.0, ((0, 64), (1, 4))),
    }


def reference(q_shared, k_shared, mixing, values, cotangent):
    score_scale = 1.0 / math.sqrt(D_QK)
    key_span = WINDOW + TOK_DEV
    block_count = TOKENS // TOK_DEV
    key_padded = jnp.concatenate([jnp.zeros((WINDOW, D_QK), jnp.bfloat16), k_shared], 0)
    value_padded = jnp.concatenate([jnp.zeros((WINDOW, HEADS * HEAD_DIM), jnp.bfloat16), values], 0)
    mixing_wide = mixing.astype(jnp.float32)
    best = lax.Precision.HIGHEST

    def one_block(carry, block_index):
        key_acc, value_acc, mixing_acc = carry
        begin_row = (block_index * TOK_DEV).astype(jnp.int32)
        queries = lax.dynamic_slice_in_dim(q_shared, begin_row, TOK_DEV, 0)
        window_keys = lax.dynamic_slice_in_dim(key_padded, begin_row, key_span, 0)
        window_values = lax.dynamic_slice_in_dim(value_padded, begin_row, key_span, 0).reshape(key_span, HEADS, HEAD_DIM)
        upstream = lax.dynamic_slice_in_dim(cotangent, begin_row, TOK_DEV, 0).reshape(TOK_DEV, HEADS, HEAD_DIM)
        mixed_query = (queries.astype(jnp.float32)[None] * mixing_wide[:, None, :]).astype(jnp.bfloat16)
        logits = jnp.einsum('hqw,kw->hqk', mixed_query.astype(jnp.float32), window_keys.astype(jnp.float32), precision=best) * score_scale
        query_pos = begin_row + jnp.arange(TOK_DEV, dtype=jnp.int32)
        key_pos = begin_row - WINDOW + jnp.arange(key_span, dtype=jnp.int32)
        key_lag = query_pos[:, None] - key_pos[None, :]
        inside = (key_pos[None, :] >= 0) & (key_lag >= 0) & (key_lag < WINDOW)
        logits = jnp.where(inside[None], logits, -jnp.inf)
        row_max = lax.optimization_barrier(jnp.max(logits, -1))
        log_norm = row_max + jnp.log(lax.optimization_barrier(jnp.sum(jnp.exp(logits - row_max[..., None]), -1)))
        weights = jnp.exp(logits - log_norm[..., None])
        slopes = jnp.einsum('qhe,khe->hqk', upstream.astype(jnp.float32), window_values.astype(jnp.float32), precision=best)
        row_delta = lax.optimization_barrier(jnp.sum(weights * slopes, -1))
        score_grad = weights * (slopes - row_delta[..., None])
        weight_half = weights.astype(jnp.bfloat16)
        grad_half = score_grad.astype(jnp.bfloat16)
        value_grad = jnp.einsum('hqk,qhe->khe', weight_half.astype(jnp.float32), upstream.astype(jnp.float32), precision=best).reshape(key_span, HEADS * HEAD_DIM)
        key_grad = jnp.einsum('hqk,hqw->kw', grad_half.astype(jnp.float32), mixed_query.astype(jnp.float32), precision=best) * score_scale
        query_grad = jnp.einsum('hqk,kw->hqw', grad_half.astype(jnp.float32), window_keys.astype(jnp.float32), precision=best) * score_scale
        query_out = jnp.einsum('hqw,hw->qw', query_grad, mixing_wide, precision=best)
        mixing_part = jnp.einsum('hqw,qw->hw', query_grad, queries.astype(jnp.float32), precision=best)
        old_keys = lax.dynamic_slice_in_dim(key_acc, begin_row, key_span, 0)
        key_acc = lax.dynamic_update_slice_in_dim(key_acc, old_keys + key_grad, begin_row, 0)
        old_values = lax.dynamic_slice_in_dim(value_acc, begin_row, key_span, 0)
        value_acc = lax.dynamic_update_slice_in_dim(value_acc, old_values + value_grad, begin_row, 0)
        return ((key_acc, value_acc, mixing_acc + mixing_part), query_out.astype(jnp.bfloat16))
    start_state = (jnp.zeros((TOKENS + WINDOW, D_QK), jnp.float32), jnp.zeros((TOKENS + WINDOW, HEADS * HEAD_DIM), jnp.float32), jnp.zeros((HEADS, D_QK), jnp.float32))
    final_state, query_blocks = lax.scan(one_block, start_state, jnp.arange(block_count, dtype=jnp.int32))
    key_acc, value_acc, mixing_acc = final_state
    d_query = query_blocks.reshape(TOKENS, D_QK)
    d_key = key_acc[WINDOW:].astype(jnp.bfloat16)
    d_values = value_acc[WINDOW:].astype(jnp.bfloat16)
    return (d_query, d_key, d_values, mixing_acc)
```

```python
import functools
import math

import jax
import jax.numpy as jnp
from jax import lax
from jax.experimental import pallas as pl
from jax.experimental.pallas import tpu as pltpu
from jax.sharding import PartitionSpec as P

GROUP = 4
HALF = 256
NEG = -1e30
LOG2E = 1.4426950408889634

NT = (((1,), (1,)), ((), ()))
NN = (((1,), (0,)), ((), ()))
TN = (((0,), (0,)), ((), ()))


def dot(a, b, dims):
    return lax.dot_general(a, b, dims, preferred_element_type=jnp.float32)


def own_kernel(scale, first_ref, mix_ref, v_ref, km_ref, c_ref, qm_ref, ko_ref, qo_ref,
               vp_ref, kpm_ref, kpo_ref, stats_ref, dqm_ref, dqo_ref, dk_ref, dv_ref,
               dmix_ref, k_all, q_all, v_all, dq_acc):
    head = pl.program_id(0)
    span = q_all.shape[0]
    tile = span // 2
    half = km_ref.shape[1]

    @pl.when(head == 0)
    def _():
        k_all[:span, :half] = kpm_ref[...]
        k_all[:span, half:] = kpo_ref[...]
        k_all[span:, :half] = km_ref[...]
        k_all[span:, half:] = ko_ref[...]
        q_all[:, :half] = qm_ref[...]
        q_all[:, half:] = qo_ref[...]
        dk_ref[...] = jnp.zeros_like(dk_ref)
        dq_acc[...] = jnp.zeros_like(dq_acc)

    v_all[:span, :] = vp_ref[...]
    v_all[span:, :] = v_ref[...]
    mix = mix_ref[0]
    is_first = first_ref[0] == 1
    row = lax.broadcasted_iota(jnp.int32, (tile, tile), 0)
    col = lax.broadcasted_iota(jnp.int32, (tile, tile), 1)
    dmix = jnp.zeros((1, mix.shape[1]), jnp.float32)
    for t in (1, 0):
        lo = t * tile
        q_f32 = q_all[lo:lo + tile, :].astype(jnp.float32)
        mq = (q_f32 * mix).astype(jnp.bfloat16)
        up = c_ref[lo:lo + tile, :]
        keys = k_all[lo:lo + 3 * tile, :]
        s = dot(keys, mq, NT) * (scale * LOG2E)
        d = dot(v_all[lo:lo + 3 * tile, :], up, NT)
        s0 = jnp.where((row > col) & jnp.logical_not(is_first), s[:tile], NEG)
        s1 = s[tile:2 * tile]
        if t == 0:
            s1 = jnp.where(is_first, NEG, s1)
        s2 = jnp.where(row <= col, s[2 * tile:], NEG)
        top = jnp.max(jnp.maximum(jnp.maximum(s0, s1), s2), 0, keepdims=True)
        p = [jnp.exp2(part - top) for part in (s0, s1, s2)]
        total = jnp.sum(p[0] + p[1] + p[2], 0, keepdims=True)
        inv = 1.0 / total
        w = [part * inv for part in p]
        ds = [d[:tile], d[tile:2 * tile], d[2 * tile:]]
        delta = jnp.sum(w[0] * ds[0] + w[1] * ds[1] + w[2] * ds[2], 0, keepdims=True)
        grad = jnp.concatenate(
            [(a * (b - delta)).astype(jnp.bfloat16) for a, b in zip(w, ds)], 0)
        stats_ref[0, 0:1, lo:lo + tile] = top + jnp.log2(total)
        stats_ref[0, 1:2, lo:lo + tile] = delta
        qg = dot(grad, keys, TN) * scale
        dq_acc[lo:lo + tile, :] += qg * mix
        dmix = dmix + jnp.sum(qg * q_f32, 0, keepdims=True)
        if t == 1:
            w_own = jnp.concatenate([w[1].astype(jnp.bfloat16), w[2].astype(jnp.bfloat16)], 0)
            dv_ref[...] = dot(w_own, up, NN)
            dk_ref[...] += dot(grad[tile:], mq, NN)
        else:
            dv_ref[:tile, :] += dot(w[2].astype(jnp.bfloat16), up, NN)
            dk_ref[:tile, :] += dot(grad[2 * tile:], mq, NN)
    dmix_ref[0] = dmix

    @pl.when(head == pl.num_programs(0) - 1)
    def _():
        dqm_ref[...] = dq_acc[:, :half]
        dqo_ref[...] = dq_acc[:, half:].astype(jnp.bfloat16)


def next_kernel(scale, mix_ref, v_ref, km_ref, ko_ref, cn_ref, qnm_ref, qno_ref, stats_ref,
                dk_ref, dv_ref, dkm_ref, dko_ref, dvo_ref, k_all, q_all, dk_acc):
    head = pl.program_id(0)
    span = q_all.shape[0]
    tile = span // 2
    half = km_ref.shape[1]

    @pl.when(head == 0)
    def _():
        k_all[:, :half] = km_ref[...]
        k_all[:, half:] = ko_ref[...]
        q_all[:, :half] = qnm_ref[...]
        q_all[:, half:] = qno_ref[...]
        dk_acc[...] = dk_ref[...]

    mix = mix_ref[0]
    row = lax.broadcasted_iota(jnp.int32, (tile, tile), 0)
    col = lax.broadcasted_iota(jnp.int32, (tile, tile), 1)
    dv = [dv_ref[:tile, :], dv_ref[tile:, :]]
    for t in (0, 1):
        lo = t * tile
        mq = (q_all[lo:lo + tile, :].astype(jnp.float32) * mix).astype(jnp.bfloat16)
        up = cn_ref[lo:lo + tile, :]
        lse = stats_ref[0, 0:1, lo:lo + tile]
        delta = stats_ref[0, 1:2, lo:lo + tile]
        s = dot(k_all[lo:, :], mq, NT) * (scale * LOG2E)
        d = dot(v_ref[lo:, :], up, NT)
        w = jnp.exp2(jnp.where(row > col, s[:tile] - lse, NEG))
        if t == 0:
            w = jnp.concatenate([w, jnp.exp2(s[tile:] - lse)], 0)
        grad = (w * (d - delta)).astype(jnp.bfloat16)
        add = dot(w.astype(jnp.bfloat16), up, NN)
        if t == 0:
            dv = [dv[0] + add[:tile], dv[1] + add[tile:]]
        else:
            dv[1] = dv[1] + add
        dk_acc[lo:, :] += dot(grad, mq, NN)
    dvo_ref[:tile, :] = dv[0].astype(jnp.bfloat16)
    dvo_ref[tile:, :] = dv[1].astype(jnp.bfloat16)

    @pl.when(head == pl.num_programs(0) - 1)
    def _():
        dkm_ref[...] = dk_acc[:, :half] * scale
        dko_ref[...] = (dk_acc[:, half:] * scale).astype(jnp.bfloat16)


def own_part(scale, first, mix, x1, kq_other, x2, kp_other):
    heads, _, width = mix.shape
    span = x1.shape[0]
    half = width // 2
    f32, b16 = jnp.float32, jnp.bfloat16
    by_head = lambda base: pl.BlockSpec((span, 128), lambda h, base=base: (0, base + h))
    fixed = lambda at: pl.BlockSpec((span, half), lambda h, at=at: (0, at))
    whole = lambda c: pl.BlockSpec((span, c), lambda h: (0, 0))
    return pl.pallas_call(
        functools.partial(own_kernel, scale),
        grid=(heads,),
        in_specs=[
            pl.BlockSpec(memory_space=pltpu.SMEM),
            pl.BlockSpec((1, 1, width), lambda h: (h, 0, 0)),
            by_head(0), fixed(2), by_head(6), fixed(5),
            fixed(0), fixed(1),
            by_head(0), fixed(2), whole(half),
        ],
        out_specs=[
            pl.BlockSpec((1, 2, span), lambda h: (h, 0, 0)),
            whole(half), whole(half), whole(width), by_head(0),
            pl.BlockSpec((1, 1, width), lambda h: (h, 0, 0)),
        ],
        out_shape=[
            jax.ShapeDtypeStruct((heads, 2, span), f32),
            jax.ShapeDtypeStruct((span, half), f32),
            jax.ShapeDtypeStruct((span, half), b16),
            jax.ShapeDtypeStruct((span, width), f32),
            jax.ShapeDtypeStruct((span, heads * 128), f32),
            jax.ShapeDtypeStruct((heads, 1, width), f32),
        ],
        scratch_shapes=[
            pltpu.VMEM((2 * span, width), b16),
            pltpu.VMEM((span, width), b16),
            pltpu.VMEM((2 * span, 128), b16),
            pltpu.VMEM((span, width), f32),
        ],
        compiler_params=pltpu.CompilerParams(vmem_limit_bytes=40 * 2**20),
        cost_estimate=pl.CostEstimate(flops=5_000_000_000, bytes_accessed=8_000_000, transcendentals=1_600_000),
    )(first, mix, x1, x1, x1, x1, kq_other, kq_other, x2, x2, kp_other)


def next_part(scale, mix, x1, kq_other, x3, qn_other, stats, dk, dv):
    heads, _, width = mix.shape
    span = x1.shape[0]
    half = width // 2
    f32, b16 = jnp.float32, jnp.bfloat16
    by_head = lambda base: pl.BlockSpec((span, 128), lambda h, base=base: (0, base + h))
    fixed = lambda at: pl.BlockSpec((span, half), lambda h, at=at: (0, at))
    whole = lambda c: pl.BlockSpec((span, c), lambda h: (0, 0))
    return pl.pallas_call(
        functools.partial(next_kernel, scale),
        grid=(heads,),
        in_specs=[
            pl.BlockSpec((1, 1, width), lambda h: (h, 0, 0)),
            by_head(0), fixed(2), fixed(0), by_head(0), fixed(2), whole(half),
            pl.BlockSpec((1, 2, span), lambda h: (h, 0, 0)),
            whole(width), by_head(0),
        ],
        out_specs=[whole(half), whole(half), by_head(0)],
        out_shape=[
            jax.ShapeDtypeStruct((span, half), f32),
            jax.ShapeDtypeStruct((span, half), b16),
            jax.ShapeDtypeStruct((span, heads * 128), b16),
        ],
        scratch_shapes=[
            pltpu.VMEM((span, width), b16),
            pltpu.VMEM((span, width), b16),
            pltpu.VMEM((span, width), f32),
        ],
        compiler_params=pltpu.CompilerParams(vmem_limit_bytes=40 * 2**20),
        cost_estimate=pl.CostEstimate(flops=2_500_000_000, bytes_accessed=7_000_000, transcendentals=800_000),
    )(mix, x1, x1, kq_other, x3, x3, qn_other, stats, dk, dv)


def per_device(q_shared, k_shared, mixing, values, cotangent):
    tok, width = q_shared.shape
    peers = lax.axis_size("seq")
    groups = [[GROUP * g + x for x in range(GROUP)] for g in range(peers // GROUP)]
    scale = 1.0 / math.sqrt(width)
    me = lax.axis_index("seq")
    place = me % GROUP
    head_at = lax.axis_index("head")
    core = head_at % 2
    y_lo = head_at // 2
    heads = mixing.shape[0] // GROUP
    cols = values.shape[1] // GROUP

    def along_groups(x, by):
        pairs = [(i, i + GROUP * by) for i in range(peers) if 0 <= i + GROUP * by < peers]
        return lax.ppermute(x, "seq", pairs)

    def core_swap(x):
        return lax.ppermute(x, "head", [(0, 1), (1, 0), (2, 3), (3, 2)])

    def trade(x):
        return lax.all_to_all(x, "seq", 0, 0, axis_index_groups=groups, tiled=True)

    def half_of(x, which):
        blocks = x.reshape(x.shape[0], 2, 2, 128)
        return lax.dynamic_index_in_dim(blocks, which, 2, keepdims=False).reshape(x.shape[0], 256)

    def split(x):
        return x.reshape(tok, GROUP, cols).transpose(1, 0, 2)

    def spread(x):
        return jnp.broadcast_to(x[None], (GROUP,) + x.shape)

    k_half = half_of(k_shared, core)
    q_half = half_of(q_shared, core)

    raw = along_groups(jnp.concatenate([values, k_half], 1), 1)
    pay1 = jnp.concatenate([split(values), spread(k_half), split(cotangent), spread(q_half)], 2)
    x1 = trade(pay1.reshape(GROUP * tok, -1))
    n_v = heads * 128
    pay2 = jnp.concatenate([split(raw[:, :GROUP * cols]), spread(raw[:, GROUP * cols:])], 2)
    x2 = trade(pay2.reshape(GROUP * tok, -1))
    x3 = along_groups(x1[:, n_v + HALF:], -1)
    kq_other = core_swap(jnp.concatenate([x1[:, n_v:n_v + HALF], x1[:, 2 * n_v + HALF:]], 1))
    kp_other = core_swap(x2[:, n_v:])
    qn_other = core_swap(x3[:, n_v:])

    mix = lax.dynamic_slice_in_dim(mixing, place * heads, heads, 0)
    mix = mix.reshape(heads, 2, 2, 128).transpose(0, 2, 1, 3)
    mix = jnp.where(core == 0, mix, mix[:, ::-1]).reshape(heads, 1, width)
    first = (me < GROUP).astype(jnp.int32).reshape(1)

    stats, dq_mine, dq_other, dk, dv, dmix = own_part(scale, first, mix, x1, kq_other, x2, kp_other)
    next_stats = along_groups(stats, -1)
    dk_mine, dk_other, dv = next_part(scale, mix, x1, kq_other, x3, qn_other, next_stats, dk, dv)

    dq_sum = dq_mine + core_swap(dq_other)
    dk_sum = dk_mine + core_swap(dk_other)
    back = trade(jnp.concatenate(
        [dv, dk_sum.astype(jnp.bfloat16), dq_sum.astype(jnp.bfloat16)], 1))
    back = back.reshape(GROUP, tok, -1)
    d_values = back[:, :, :n_v].transpose(1, 0, 2).reshape(tok, GROUP * n_v)
    sums = jnp.sum(back[:, :, n_v:].astype(jnp.float32), 0).reshape(tok, 2, 2, 128)
    keep = lax.dynamic_index_in_dim(sums, y_lo, 2, keepdims=False)
    give = lax.dynamic_index_in_dim(sums, 1 - y_lo, 2, keepdims=False)
    got = lax.ppermute(give.reshape(tok, 256), "head", [(0, 2), (1, 3), (2, 0), (3, 1)])
    done = (keep.reshape(tok, 256) + got).astype(jnp.bfloat16)
    d_key = done[:, :128]
    d_query = done[:, 128:]

    dmix = dmix.reshape(heads, width)
    step = GROUP
    while step < peers:
        dmix = dmix + lax.ppermute(dmix, "seq", [(i, i ^ step) for i in range(peers)])
        step *= 2
    wide = lax.dynamic_update_slice_in_dim(
        jnp.zeros((GROUP * heads, width), jnp.float32), dmix, place * heads, 0)
    for step in (1, 2):
        wide = wide + lax.ppermute(wide, "seq", [(i, i ^ step) for i in range(peers)])
    wide = wide.reshape(GROUP * heads, 2, 2, 128)
    wide = jnp.where(core == 0, wide, wide[:, ::-1])
    d_mixing = wide.transpose(0, 2, 1, 3).reshape(GROUP * heads, width)
    return d_query, d_key, d_values, d_mixing


def solution(mesh):
    placed = (P("seq", None), P("seq", None), P("head", None), P("seq", "head"), P("seq", "head"))
    return jax.shard_map(
        per_device,
        mesh=mesh,
        in_specs=placed,
        out_specs=(P("seq", "head"), P("seq", "head"), P("seq", "head"), P("head", None)),
        check_vma=False,
    )
```

```python
import functools
import math

import jax
import jax.numpy as jnp
from jax import lax
from jax.experimental import pallas as pl
from jax.experimental.pallas import tpu as pltpu
from jax.sharding import PartitionSpec as P

GROUP = 4
HALF = 256
NEG = -1e30
LOG2E = 1.4426950408889634

NT = (((1,), (1,)), ((), ()))
NN = (((1,), (0,)), ((), ()))
TN = (((0,), (0,)), ((), ()))


def dot(a, b, dims):
    return lax.dot_general(a, b, dims, preferred_element_type=jnp.float32)


def blocks_of(at_ref):
    core = at_ref[0]
    return core, 2 + core, 1 - core, 3 - core


def rows_from(at_ref, by):
    src = lax.rem(at_ref[1] + GROUP - by, GROUP)
    return pl.ds(pl.multiple_of(src * 128, 128), 128)


def scores_kernel(scale, at_ref, mix_ref, v_ref, km_ref, c_ref, qm_ref, ko_ref, qo_ref,
                  vp0_ref, vp1_ref, vp2_ref, vp3_ref, kpm_ref, kpo_ref,
                  stats_ref, grad_ref, w_ref, k_all_ref, q_all_ref, k_all, q_all, v_all):
    head = pl.program_id(0)
    span = q_all.shape[0]
    tile = span // 2
    half = km_ref.shape[1]

    @pl.when(head == 0)
    def _():
        k_all[:span, :half] = kpm_ref[...]
        k_all[:span, half:] = kpo_ref[...]
        k_all[span:, :half] = km_ref[...]
        k_all[span:, half:] = ko_ref[...]
        q_all[:, :half] = qm_ref[...]
        q_all[:, half:] = qo_ref[...]
        k_all_ref[...] = k_all[...]
        q_all_ref[...] = q_all[...]

    for e, ref in enumerate((vp0_ref, vp1_ref, vp2_ref, vp3_ref)):
        v_all[rows_from(at_ref, e), :] = ref[...]
    v_all[span:, :] = v_ref[...]
    mix = mix_ref[0]
    is_first = at_ref[2] == 0
    row = lax.broadcasted_iota(jnp.int32, (tile, tile), 0)
    col = lax.broadcasted_iota(jnp.int32, (tile, tile), 1)
    for t in (0, 1):
        lo = t * tile
        mq = (q_all[lo:lo + tile, :].astype(jnp.float32) * mix).astype(jnp.bfloat16)
        up = c_ref[lo:lo + tile, :]
        s = dot(k_all[lo:lo + 3 * tile, :], mq, NT) * (scale * LOG2E)
        d = dot(v_all[lo:lo + 3 * tile, :], up, NT)
        s0 = jnp.where((row > col) & jnp.logical_not(is_first), s[:tile], NEG)
        s1 = s[tile:2 * tile]
        if t == 0:
            s1 = jnp.where(is_first, NEG, s1)
        s2 = jnp.where(row <= col, s[2 * tile:], NEG)
        top = jnp.max(jnp.maximum(jnp.maximum(s0, s1), s2), 0, keepdims=True)
        p = [jnp.exp2(part - top) for part in (s0, s1, s2)]
        total = jnp.sum(p[0] + p[1] + p[2], 0, keepdims=True)
        inv = 1.0 / total
        ds = [d[:tile], d[tile:2 * tile], d[2 * tile:]]
        delta = jnp.sum(p[0] * ds[0] + p[1] * ds[1] + p[2] * ds[2], 0, keepdims=True) * inv
        stats_ref[0, 0:1, lo:lo + tile] = top + jnp.log2(total)
        stats_ref[0, 1:2, lo:lo + tile] = delta
        for i in range(3):
            w = p[i] * inv
            grad_ref[0, t, i * tile:(i + 1) * tile, :] = (w * (ds[i] - delta)).astype(jnp.bfloat16)
            if i == 2:
                w_ref[0, 2 * t, :, :] = w.astype(jnp.bfloat16)
            if i == 1 and t == 1:
                w_ref[0, 1, :, :] = w.astype(jnp.bfloat16)


def query_kernel(scale, at_ref, mix_ref, k_ref, q_ref, grad_ref, dqm_ref, dqo_ref, dmix_ref, dq_acc):
    head = pl.program_id(0)
    span, width = q_ref.shape
    tile = span // 2

    @pl.when(head == 0)
    def _():
        dq_acc[...] = jnp.zeros_like(dq_acc)

    mix = mix_ref[0]
    dmix = jnp.zeros((1, width), jnp.float32)
    for t in (0, 1):
        lo = t * tile
        qg = dot(grad_ref[0, t], k_ref[lo:lo + 3 * tile, :], TN) * scale
        dq_acc[lo:lo + tile, :] += qg * mix
        dmix = dmix + jnp.sum(qg * q_ref[lo:lo + tile, :].astype(jnp.float32), 0, keepdims=True)
    for m, block in enumerate(blocks_of(at_ref)):
        dmix_ref[0, :, pl.ds(pl.multiple_of(block * 128, 128), 128)] = dmix[:, m * 128:(m + 1) * 128]

    @pl.when(head == pl.num_programs(0) - 1)
    def _():
        dqm_ref[...] = dq_acc[:, :width // 2]
        dqo_ref[...] = dq_acc[:, width // 2:].astype(jnp.bfloat16)


def key_kernel(mix_ref, c_ref, q_ref, grad_ref, w_ref, dk_ref, dv_ref):
    head = pl.program_id(0)
    span = q_ref.shape[0]
    tile = span // 2

    @pl.when(head == 0)
    def _():
        dk_ref[...] = jnp.zeros_like(dk_ref)

    mix = mix_ref[0]
    mq = (q_ref[...].astype(jnp.float32) * mix).astype(jnp.bfloat16)
    dk_ref[...] += dot(grad_ref[0, 1, tile:, :], mq[tile:], NN)
    dk_ref[:tile, :] += dot(grad_ref[0, 0, 2 * tile:, :], mq[:tile], NN)
    dv_ref[tile:, :] = dot(w_ref[0, 2], c_ref[tile:, :], NN)
    dv_ref[:tile, :] = dot(w_ref[0, 1], c_ref[tile:, :], NN) + dot(w_ref[0, 0], c_ref[:tile, :], NN)


def next_kernel(scale, mix_ref, v_ref, km_ref, ko_ref, cn_ref, qnm_ref, qno_ref, stats_ref,
                dk_ref, dv_ref, dkm_ref, dko_ref, dvo_ref, k_all, q_all, dk_acc):
    head = pl.program_id(0)
    span = q_all.shape[0]
    tile = span // 2
    half = km_ref.shape[1]

    @pl.when(head == 0)
    def _():
        k_all[:, :half] = km_ref[...]
        k_all[:, half:] = ko_ref[...]
        q_all[:, :half] = qnm_ref[...]
        q_all[:, half:] = qno_ref[...]
        dk_acc[...] = dk_ref[...]

    mix = mix_ref[0]
    row = lax.broadcasted_iota(jnp.int32, (tile, tile), 0)
    col = lax.broadcasted_iota(jnp.int32, (tile, tile), 1)
    dv = [dv_ref[:tile, :], dv_ref[tile:, :]]
    for t in (0, 1):
        lo = t * tile
        mq = (q_all[lo:lo + tile, :].astype(jnp.float32) * mix).astype(jnp.bfloat16)
        up = cn_ref[lo:lo + tile, :]
        lse = stats_ref[0, 0:1, lo:lo + tile]
        delta = stats_ref[0, 1:2, lo:lo + tile]
        s = dot(k_all[lo:, :], mq, NT) * (scale * LOG2E)
        d = dot(v_ref[lo:, :], up, NT)
        w = jnp.exp2(jnp.where(row > col, s[:tile] - lse, NEG))
        if t == 0:
            w = jnp.concatenate([w, jnp.exp2(s[tile:] - lse)], 0)
        grad = (w * (d - delta)).astype(jnp.bfloat16)
        add = dot(w.astype(jnp.bfloat16), up, NN)
        if t == 0:
            dv = [dv[0] + add[:tile], dv[1] + add[tile:]]
        else:
            dv[1] = dv[1] + add
        dk_acc[lo:, :] += dot(grad, mq, NN)
    dvo_ref[:tile, :] = dv[0].astype(jnp.bfloat16)
    dvo_ref[tile:, :] = dv[1].astype(jnp.bfloat16)

    @pl.when(head == pl.num_programs(0) - 1)
    def _():
        dkm_ref[...] = dk_acc[:, :half] * scale
        dko_ref[...] = (dk_acc[:, half:] * scale).astype(jnp.bfloat16)


def load_kernel(at_ref, v_ref, c_ref, k_ref, q_ref, own0_ref, own1_ref, own2_ref, own3_ref,
                ahead_ref, k_in, q_in, sems):
    core, place = at_ref[0], at_ref[1]
    wide = v_ref.shape[1]
    cols = wide // GROUP
    pending = []

    def send(src, dst):
        copy = pltpu.make_async_copy(src, dst, sems.at[len(pending)])
        copy.start()
        pending.append(copy)
        return copy

    shared = [send(k_ref, k_in), send(q_ref, q_in)]
    send(v_ref, ahead_ref.at[:, :wide])
    owns = (own0_ref, own1_ref, own2_ref, own3_ref)
    for e, own in enumerate(owns):
        src = pl.ds(pl.multiple_of(lax.rem(place + e, GROUP) * cols, 128), cols)
        send(v_ref.at[:, src], own.at[:, :cols])
        send(c_ref.at[:, src], own.at[:, cols + 2 * HALF:])
    for copy in shared:
        copy.wait()
    for m in range(2):
        src = pl.ds(pl.multiple_of((2 * m + core) * 128, 128), 128)
        k_block, q_block = k_in[:, src], q_in[:, src]
        ahead_ref[:, wide + m * 128:wide + (m + 1) * 128] = k_block
        for own in owns:
            own[:, cols + m * 128:cols + (m + 1) * 128] = k_block
            own[:, cols + HALF + m * 128:cols + HALF + (m + 1) * 128] = q_block
    for copy in pending[2:]:
        copy.wait()


def split_kernel(at_ref, raw_ref, *hops):
    cols = hops[0].shape[1] - HALF
    for e, hop in enumerate(hops):
        src = lax.rem(at_ref[1] + e, GROUP) * cols
        hop[:, :cols] = raw_ref[:, pl.ds(pl.multiple_of(src, 128), cols)]
        hop[:, cols:] = raw_ref[:, GROUP * cols:]


def gather_kernel(at_ref, p0_ref, p1_ref, p2_ref, p3_ref, vk_ref, qc_ref, kq_ref):
    half = vk_ref.shape[1]
    for e, ref in enumerate((p0_ref, p1_ref, p2_ref, p3_ref)):
        rows = rows_from(at_ref, e)
        vk_ref[rows, :] = ref[:, :half]
        qc_ref[rows, :] = ref[:, half:]
        kq_ref[rows, :] = ref[:, half - HALF:half + HALF]


def collect_kernel(at_ref, mixing_ref, k0_ref, k1_ref, k2_ref, k3_ref, k_ref, mix_ref):
    core, place = at_ref[0], at_ref[1]
    for e, ref in enumerate((k0_ref, k1_ref, k2_ref, k3_ref)):
        k_ref[rows_from(at_ref, e), :] = ref[...]
    for h in range(mix_ref.shape[0]):
        row = mixing_ref[pl.ds(place * mix_ref.shape[0] + h, 1), :]
        blocks = [row[:, i * 128:(i + 1) * 128] for i in range(4)]
        for m, (even, odd) in enumerate(((0, 1), (2, 3), (1, 0), (3, 2))):
            mix_ref[h, :, m * 128:(m + 1) * 128] = jnp.where(core == 0, blocks[even], blocks[odd])


def pack_kernel(at_ref, dv_ref, dk_ref, dk_got_ref, dq_ref, dq_got_ref, *outs):
    cols = dv_ref.shape[1]
    for e, out in enumerate(outs):
        dest = lax.rem(at_ref[1] + e, GROUP)
        rows = pl.ds(pl.multiple_of(dest * 128, 128), 128)
        out[:, :cols] = dv_ref[rows, :]
        dk = dk_ref[rows, :] + dk_got_ref[rows, :].astype(jnp.float32)
        dq = dq_ref[rows, :] + dq_got_ref[rows, :].astype(jnp.float32)
        out[:, cols:cols + HALF] = dk.astype(jnp.bfloat16)
        out[:, cols + HALF:] = dq.astype(jnp.bfloat16)


def sums_kernel(at_ref, *refs):
    parts, (keep_ref, give_ref) = refs[:-2], refs[-2:]
    wide = parts[0].shape[1] - 2 * HALF
    y_lo = at_ref[3]
    for m in range(2):
        for ref, which in ((keep_ref, y_lo), (give_ref, 1 - y_lo)):
            src = pl.ds(pl.multiple_of(wide + m * HALF + which * 128, 128), 128)
            total = parts[0][:, src].astype(jnp.float32)
            for part in parts[1:]:
                total = total + part[:, src].astype(jnp.float32)
            ref[:, m * 128:(m + 1) * 128] = total


def values_kernel(at_ref, *refs):
    out = refs[-1]
    cols = out.shape[1] // GROUP
    for e, ref in enumerate(refs[:-1]):
        src = lax.rem(at_ref[1] + GROUP - e, GROUP) * cols
        out[:, pl.ds(pl.multiple_of(src, 128), cols)] = ref[:, :cols]


def last_kernel(keep_ref, got_ref, dk_ref, dq_ref):
    done = (keep_ref[...] + got_ref[...]).astype(jnp.bfloat16)
    dk_ref[...] = done[:, :128]
    dq_ref[...] = done[:, 128:]


def mixing_kernel(at_ref, *refs):
    out = refs[-1]
    for e, ref in enumerate(refs[:-1]):
        src = lax.rem(at_ref[1] + GROUP - e, GROUP)
        for h in range(ref.shape[0]):
            out[pl.ds(src * ref.shape[0] + h, 1), :] = ref[h:h + 1, :]


SMEM = pl.BlockSpec(memory_space=pltpu.SMEM)
VMEM = pl.BlockSpec(memory_space=pltpu.VMEM)
ANY = pl.BlockSpec(memory_space=pl.ANY)
F32, B16 = jnp.float32, jnp.bfloat16


def call(body, grid, ins, outs, scratch, args, micros, vmem=40):
    return pl.pallas_call(
        body,
        grid=grid,
        in_specs=ins,
        out_specs=[spec for spec, _, _ in outs],
        out_shape=[jax.ShapeDtypeStruct(shape, kind) for _, shape, kind in outs],
        scratch_shapes=scratch,
        compiler_params=pltpu.CompilerParams(vmem_limit_bytes=vmem * 2**20),
        cost_estimate=pl.CostEstimate(
            flops=int(micros * 1e9), bytes_accessed=1_000_000, transcendentals=0),
    )(*args)


def fixed(shape, *at):
    return pl.BlockSpec(shape, lambda h: at or (0,) * len(shape))


def by_head(rows, base=0):
    return pl.BlockSpec((rows, 128), lambda h: (0, base + h))


def head_first(*shape):
    return pl.BlockSpec((1,) + shape, lambda h: (h,) + (0,) * len(shape))


def per_device(q_shared, k_shared, mixing, values, cotangent):
    tok, width = q_shared.shape
    peers = lax.axis_size("seq")
    scale = 1.0 / math.sqrt(width)
    me = lax.axis_index("seq")
    head_at = lax.axis_index("head")
    heads = mixing.shape[0] // GROUP
    n_v = heads * 128
    span = GROUP * tok
    at = jnp.stack([lax.rem(head_at, 2), lax.rem(me, GROUP), lax.div(me, GROUP), lax.div(head_at, 2)])

    def to_group(x, by):
        pairs = [(i, i + GROUP * by) for i in range(peers) if 0 <= i + GROUP * by < peers]
        return lax.ppermute(x, "seq", pairs)

    def turn(x, by):
        pairs = [(i, i - i % GROUP + (i + by) % GROUP) for i in range(peers)]
        return lax.ppermute(x, "seq", pairs)

    def turns(parts):
        return [parts[0]] + [turn(part, e) for e, part in enumerate(parts) if e]

    def core_swap(x):
        return lax.ppermute(x, "head", [(0, 1), (1, 0), (2, 3), (3, 2)])

    whole = lambda x: fixed(x.shape)
    wide = n_v + HALF
    *own, ahead = call(
        load_kernel, (), [SMEM] + [ANY] * 4,
        [(VMEM, (tok, 2 * wide), B16)] * GROUP + [(VMEM, (tok, GROUP * n_v + HALF), B16)],
        [pltpu.VMEM((tok, width), B16)] * 2 + [pltpu.SemaphoreType.DMA((11,))],
        (at, values, cotangent, k_shared, q_shared), 3, vmem=56)
    ahead = to_group(ahead, 1)
    own = turns(own)
    before = call(split_kernel, (1,), [SMEM, whole(ahead)],
                  [(fixed((tok, wide)), (tok, wide), B16)] * GROUP, [], (at, ahead), 1)
    before = list(before)
    own[0], before[0] = lax.optimization_barrier((own[0], before[0]))
    before = turns(before)
    vk, qc, kq = call(
        gather_kernel, (1,), [SMEM] + [whole(own[0])] * GROUP,
        [(fixed((span, wide)), (span, wide), B16)] * 2
        + [(fixed((span, 2 * HALF)), (span, 2 * HALF), B16)], [], (at, *own), 8)
    x3 = to_group(qc, -1)
    kq_other = core_swap(kq)
    kp, mix = call(
        collect_kernel, (1,),
        [SMEM, fixed((GROUP * heads, width))] + [fixed((tok, HALF), 0, 2)] * GROUP,
        [(fixed((span, HALF)), (span, HALF), B16),
         (fixed((heads, 1, width)), (heads, 1, width), F32)],
        [], (at, mixing, *before), 1)
    kp_other = core_swap(kp)

    stats, grad, w, k_all, q_all = call(
        functools.partial(scores_kernel, scale), (heads,),
        [SMEM, head_first(1, width), by_head(span), fixed((span, HALF), 0, 2), by_head(span, 2),
         fixed((span, HALF), 0, 0), fixed((span, HALF), 0, 0), fixed((span, HALF), 0, 1)]
        + [by_head(tok)] * GROUP + [fixed((span, HALF))] * 2,
        [(head_first(2, span), (heads, 2, span), F32),
         (head_first(2, 768, 256), (heads, 2, 768, 256), B16),
         (head_first(3, 256, 256), (heads, 3, 256, 256), B16),
         (fixed((2 * span, width)), (2 * span, width), B16),
         (fixed((span, width)), (span, width), B16)],
        [pltpu.VMEM((2 * span, width), B16), pltpu.VMEM((span, width), B16),
         pltpu.VMEM((2 * span, 128), B16)],
        (at, mix, vk, vk, qc, qc, kq_other, kq_other, *before, kp, kp_other), 0.1)
    next_stats = to_group(stats, -1)
    dq_mine, dq_other, dmix = call(
        functools.partial(query_kernel, scale), (heads,),
        [SMEM, head_first(1, width), fixed((2 * span, width)), fixed((span, width)),
         head_first(2, 768, 256)],
        [(fixed((span, HALF)), (span, HALF), F32), (fixed((span, HALF)), (span, HALF), B16),
         (head_first(1, width), (heads, 1, width), F32)],
        [pltpu.VMEM((span, width), F32)],
        (at, mix, k_all, q_all, grad), 0.3)

    def from_peer(x, by):
        return lax.ppermute(x, "seq", [(i, i ^ by) for i in range(peers)])

    def exchange(x, a, b):
        return (x + from_peer(x, a)) + (from_peer(x, b) + from_peer(x, a ^ b))

    dk, dv = call(
        key_kernel, (heads,),
        [head_first(1, width), by_head(span, 2), fixed((span, width)),
         head_first(2, 768, 256), head_first(3, 256, 256)],
        [(fixed((span, width)), (span, width), F32), (by_head(span), (span, n_v), F32)],
        [], (mix, qc, q_all, grad, w), 0.3)
    x3, dk = lax.optimization_barrier((x3, dk))
    qn_other = core_swap(x3[:, :HALF])
    dk_mine, dk_other, dv = call(
        functools.partial(next_kernel, scale), (heads,),
        [head_first(1, width), by_head(span), fixed((span, HALF), 0, 2),
         fixed((span, HALF), 0, 0), by_head(span, 2), fixed((span, HALF), 0, 0),
         fixed((span, HALF)), head_first(2, span), fixed((span, width)), by_head(span)],
        [(fixed((span, HALF)), (span, HALF), F32), (fixed((span, HALF)), (span, HALF), B16),
         (by_head(span), (span, n_v), B16)],
        [pltpu.VMEM((span, width), B16), pltpu.VMEM((span, width), B16),
         pltpu.VMEM((span, width), F32)],
        (mix, vk, vk, kq_other, x3, x3, qn_other, next_stats, dk, dv), 6)
    dk_other, dq_other, dmix = lax.optimization_barrier((dk_other, dq_other, dmix))
    dmix = exchange(dmix.reshape(heads, width), GROUP, 2 * GROUP)

    dk_got, dq_got = core_swap(dk_other), core_swap(dq_other)
    back = call(
        pack_kernel, (1,), [SMEM, whole(dv), whole(dk_mine), whole(dk_got), whole(dq_mine), whole(dq_got)],
        [(fixed((tok, n_v + 2 * HALF)), (tok, n_v + 2 * HALF), B16)] * GROUP, [],
        (at, dv, dk_mine, dk_got, dq_mine, dq_got), 1)
    back = turns(back)
    keep, give = call(sums_kernel, (1,), [SMEM] + [whole(back[0])] * GROUP,
                      [(fixed((tok, HALF)), (tok, HALF), F32)] * 2, [], (at, *back), 1)
    dmix = exchange(dmix, 4 * GROUP, 8 * GROUP)
    dmix, give = lax.optimization_barrier((dmix, give))
    got = lax.ppermute(give, "head", [(0, 2), (1, 3), (2, 0), (3, 1)])
    (d_values,) = call(values_kernel, (1,), [SMEM] + [whole(back[0])] * GROUP,
                       [(fixed((tok, GROUP * n_v)), (tok, GROUP * n_v), B16)], [], (at, *back), 1)
    d_key, d_query = call(last_kernel, (1,), [whole(keep)] * 2,
                          [(fixed((tok, 128)), (tok, 128), B16)] * 2, [], (keep, got), 1)

    dmix = turns([dmix] * GROUP)
    (d_mixing,) = call(mixing_kernel, (1,), [SMEM] + [whole(dmix[0])] * GROUP,
                       [(fixed((GROUP * heads, width)), (GROUP * heads, width), F32)], [], (at, *dmix), 1)
    return d_query, d_key, d_values, d_mixing


def solution(mesh):
    placed = (P("seq", None), P("seq", None), P("head", None), P("seq", "head"), P("seq", "head"))
    return jax.shard_map(
        per_device,
        mesh=mesh,
        in_specs=placed,
        out_specs=(P("seq", "head"), P("seq", "head"), P("seq", "head"), P("head", None)),
        check_vma=False,
    )
```

```python
import functools
import math

import jax
import jax.numpy as jnp
from jax import lax
from jax.experimental import pallas as pl
from jax.experimental.pallas import tpu as pltpu
from jax.sharding import PartitionSpec as P

GROUP = 4
HALF = 256
NEG = -1e30
LOG2E = 1.4426950408889634

NT = (((1,), (1,)), ((), ()))
NN = (((1,), (0,)), ((), ()))
TN = (((0,), (0,)), ((), ()))


def dot(a, b, dims):
    return lax.dot_general(a, b, dims, preferred_element_type=jnp.float32)


def blocks_of(at_ref):
    core = at_ref[0]
    return core, 2 + core, 1 - core, 3 - core


def rows_from(at_ref, by):
    src = lax.rem(at_ref[1] + GROUP - by, GROUP)
    return pl.ds(pl.multiple_of(src * 128, 128), 128)


def scores_kernel(scale, at_ref, mix_ref, v_ref, km_ref, c_ref, qm_ref, ko_ref, qo_ref,
                  vp0_ref, vp1_ref, vp2_ref, vp3_ref, kpm_ref, kpo_ref,
                  stats_ref, grad_ref, w_ref, k_all_ref, q_all_ref, k_all, q_all, v_all):
    head = pl.program_id(0)
    span = q_all.shape[0]
    tile = span // 2
    half = km_ref.shape[1]

    @pl.when(head == 0)
    def _():
        k_all[:span, :half] = kpm_ref[...]
        k_all[:span, half:] = kpo_ref[...]
        k_all[span:, :half] = km_ref[...]
        k_all[span:, half:] = ko_ref[...]
        q_all[:, :half] = qm_ref[...]
        q_all[:, half:] = qo_ref[...]
        k_all_ref[...] = k_all[...]
        q_all_ref[...] = q_all[...]

    for e, ref in enumerate((vp0_ref, vp1_ref, vp2_ref, vp3_ref)):
        v_all[rows_from(at_ref, e), :] = ref[...]
    v_all[span:, :] = v_ref[...]
    mix = mix_ref[0]
    is_first = at_ref[2] == 0
    row = lax.broadcasted_iota(jnp.int32, (tile, tile), 0)
    col = lax.broadcasted_iota(jnp.int32, (tile, tile), 1)
    for t in (0, 1):
        lo = t * tile
        mq = (q_all[lo:lo + tile, :].astype(jnp.float32) * mix).astype(jnp.bfloat16)
        up = c_ref[lo:lo + tile, :]
        s = dot(k_all[lo:lo + 3 * tile, :], mq, NT) * (scale * LOG2E)
        d = dot(v_all[lo:lo + 3 * tile, :], up, NT)
        s0 = jnp.where((row > col) & jnp.logical_not(is_first), s[:tile], NEG)
        s1 = s[tile:2 * tile]
        if t == 0:
            s1 = jnp.where(is_first, NEG, s1)
        s2 = jnp.where(row <= col, s[2 * tile:], NEG)
        top = jnp.max(jnp.maximum(jnp.maximum(s0, s1), s2), 0, keepdims=True)
        p = [jnp.exp2(part - top) for part in (s0, s1, s2)]
        total = jnp.sum(p[0] + p[1] + p[2], 0, keepdims=True)
        inv = 1.0 / total
        ds = [d[:tile], d[tile:2 * tile], d[2 * tile:]]
        delta = jnp.sum(p[0] * ds[0] + p[1] * ds[1] + p[2] * ds[2], 0, keepdims=True) * inv
        stats_ref[0, 0:1, lo:lo + tile] = top + jnp.log2(total)
        stats_ref[0, 1:2, lo:lo + tile] = delta
        for i in range(3):
            w = p[i] * inv
            grad_ref[0, t, i * tile:(i + 1) * tile, :] = (w * (ds[i] - delta)).astype(jnp.bfloat16)
            if i == 2:
                w_ref[0, 2 * t, :, :] = w.astype(jnp.bfloat16)
            if i == 1 and t == 1:
                w_ref[0, 1, :, :] = w.astype(jnp.bfloat16)


def query_kernel(scale, at_ref, mix_ref, k_ref, q_ref, grad_ref, dqm_ref, dqo_ref, dmix_ref, dq_acc):
    head = pl.program_id(0)
    span, width = q_ref.shape
    tile = span // 2

    @pl.when(head == 0)
    def _():
        dq_acc[...] = jnp.zeros_like(dq_acc)

    mix = mix_ref[0]
    dmix = jnp.zeros((1, width), jnp.float32)
    for t in (0, 1):
        lo = t * tile
        qg = dot(grad_ref[0, t], k_ref[lo:lo + 3 * tile, :], TN) * scale
        dq_acc[lo:lo + tile, :] += qg * mix
        dmix = dmix + jnp.sum(qg * q_ref[lo:lo + tile, :].astype(jnp.float32), 0, keepdims=True)
    for m, block in enumerate(blocks_of(at_ref)):
        dmix_ref[0, :, pl.ds(pl.multiple_of(block * 128, 128), 128)] = dmix[:, m * 128:(m + 1) * 128]

    @pl.when(head == pl.num_programs(0) - 1)
    def _():
        dqm_ref[...] = dq_acc[:, :width // 2]
        dqo_ref[...] = dq_acc[:, width // 2:].astype(jnp.bfloat16)


def key_kernel(mix_ref, c_ref, q_ref, grad_ref, w_ref, dk_ref, dv_ref):
    head = pl.program_id(0)
    span = q_ref.shape[0]
    tile = span // 2

    @pl.when(head == 0)
    def _():
        dk_ref[...] = jnp.zeros_like(dk_ref)

    mix = mix_ref[0]
    mq = (q_ref[...].astype(jnp.float32) * mix).astype(jnp.bfloat16)
    dk_ref[...] += dot(grad_ref[0, 1, tile:, :], mq[tile:], NN)
    dk_ref[:tile, :] += dot(grad_ref[0, 0, 2 * tile:, :], mq[:tile], NN)
    dv_ref[tile:, :] = dot(w_ref[0, 2], c_ref[tile:, :], NN)
    dv_ref[:tile, :] = dot(w_ref[0, 1], c_ref[tile:, :], NN) + dot(w_ref[0, 0], c_ref[:tile, :], NN)


def next_kernel(scale, at_ref, mix_ref, v_ref, km_ref, ko_ref, cn_ref, qnm_ref, qno_ref, stats_ref,
                dk_ref, dv_ref, dkm_ref, dko_ref, dvo_ref, k_all, q_all, dk_acc):
    head = pl.program_id(0)
    span = q_all.shape[0]
    tile = span // 2
    half = km_ref.shape[1]

    @pl.when(head == 0)
    def _():
        k_all[:, :half] = km_ref[...]
        k_all[:, half:] = ko_ref[...]
        q_all[:, :half] = qnm_ref[...]
        q_all[:, half:] = qno_ref[...]
        dk_acc[...] = dk_ref[...]

    mix = mix_ref[0]
    row = lax.broadcasted_iota(jnp.int32, (tile, tile), 0)
    col = lax.broadcasted_iota(jnp.int32, (tile, tile), 1)
    is_last = at_ref[4] == 1
    seen = (row > col) & jnp.logical_not(is_last)
    dv = [dv_ref[:tile, :], dv_ref[tile:, :]]
    for t in (0, 1):
        lo = t * tile
        mq = (q_all[lo:lo + tile, :].astype(jnp.float32) * mix).astype(jnp.bfloat16)
        up = cn_ref[lo:lo + tile, :]
        lse = stats_ref[0, 0:1, lo:lo + tile]
        delta = stats_ref[0, 1:2, lo:lo + tile]
        s = dot(k_all[lo:, :], mq, NT) * (scale * LOG2E)
        d = dot(v_ref[lo:, :], up, NT)
        w = jnp.exp2(jnp.where(seen, s[:tile] - lse, NEG))
        if t == 0:
            w = jnp.concatenate([w, jnp.exp2(jnp.where(is_last, NEG, s[tile:] - lse))], 0)
        grad = (w * (d - delta)).astype(jnp.bfloat16)
        add = dot(w.astype(jnp.bfloat16), up, NN)
        if t == 0:
            dv = [dv[0] + add[:tile], dv[1] + add[tile:]]
        else:
            dv[1] = dv[1] + add
        dk_acc[lo:, :] += dot(grad, mq, NN)
    dvo_ref[:tile, :] = dv[0].astype(jnp.bfloat16)
    dvo_ref[tile:, :] = dv[1].astype(jnp.bfloat16)

    @pl.when(head == pl.num_programs(0) - 1)
    def _():
        dkm_ref[...] = dk_acc[:, :half] * scale
        dko_ref[...] = (dk_acc[:, half:] * scale).astype(jnp.bfloat16)


def load_kernel(at_ref, v_ref, c_ref, k_ref, q_ref, own0_ref, own1_ref, own2_ref, own3_ref,
                ahead_ref, k_in, q_in, sems):
    core, place = at_ref[0], at_ref[1]
    wide = v_ref.shape[1]
    cols = wide // GROUP
    pending = []

    def send(src, dst):
        copy = pltpu.make_async_copy(src, dst, sems.at[len(pending)])
        copy.start()
        pending.append(copy)
        return copy

    shared = [send(k_ref, k_in), send(q_ref, q_in)]
    owns = (own0_ref, own1_ref, own2_ref, own3_ref)
    for e, own in enumerate(owns):
        src = pl.ds(pl.multiple_of(lax.rem(place + e, GROUP) * cols, 128), cols)
        send(v_ref.at[:, src], own.at[:, :cols])
        send(c_ref.at[:, src], own.at[:, cols + 2 * HALF:])
    for copy in shared:
        copy.wait()
    for m in range(2):
        src = pl.ds(pl.multiple_of((2 * m + core) * 128, 128), 128)
        k_block, q_block = k_in[:, src], q_in[:, src]
        ahead_ref[:, m * 128:(m + 1) * 128] = k_block
        for own in owns:
            own[:, cols + m * 128:cols + (m + 1) * 128] = k_block
            own[:, cols + HALF + m * 128:cols + HALF + (m + 1) * 128] = q_block
    for copy in pending[2:]:
        copy.wait()


def split_kernel(at_ref, raw_ref, k_ref, *hops):
    cols = hops[0].shape[1] - HALF
    for e, hop in enumerate(hops):
        src = lax.rem(at_ref[1] + e, GROUP) * cols
        hop[:, :cols] = raw_ref[:, pl.ds(pl.multiple_of(src, 128), cols)]
        hop[:, cols:] = k_ref[...]


def gather_kernel(at_ref, p0_ref, p1_ref, p2_ref, p3_ref, vk_ref, q_ref, c_ref, kq_ref):
    half = vk_ref.shape[1]
    for e, ref in enumerate((p0_ref, p1_ref, p2_ref, p3_ref)):
        rows = rows_from(at_ref, e)
        vk_ref[rows, :] = ref[:, :half]
        q_ref[rows, :] = ref[:, half:half + HALF]
        c_ref[rows, :] = ref[:, half + HALF:]
        kq_ref[rows, :] = ref[:, half - HALF:half + HALF]


def collect_kernel(at_ref, mixing_ref, k0_ref, k1_ref, k2_ref, k3_ref, k_ref, mix_ref):
    core, place = at_ref[0], at_ref[1]
    for e, ref in enumerate((k0_ref, k1_ref, k2_ref, k3_ref)):
        k_ref[rows_from(at_ref, e), :] = ref[...]
    for h in range(mix_ref.shape[0]):
        row = mixing_ref[pl.ds(place * mix_ref.shape[0] + h, 1), :]
        blocks = [row[:, i * 128:(i + 1) * 128] for i in range(4)]
        for m, (even, odd) in enumerate(((0, 1), (2, 3), (1, 0), (3, 2))):
            mix_ref[h, :, m * 128:(m + 1) * 128] = jnp.where(core == 0, blocks[even], blocks[odd])


def pack_kernel(at_ref, dv_ref, dk_ref, dk_got_ref, dq_ref, dq_got_ref, *outs):
    cols = dv_ref.shape[1]
    for e, out in enumerate(outs):
        dest = lax.rem(at_ref[1] + e, GROUP)
        rows = pl.ds(pl.multiple_of(dest * 128, 128), 128)
        out[:, :cols] = dv_ref[rows, :]
        dk = dk_ref[rows, :] + dk_got_ref[rows, :].astype(jnp.float32)
        dq = dq_ref[rows, :] + dq_got_ref[rows, :].astype(jnp.float32)
        out[:, cols:cols + HALF] = dk.astype(jnp.bfloat16)
        out[:, cols + HALF:] = dq.astype(jnp.bfloat16)


def sums_kernel(at_ref, *refs):
    parts, (keep_ref, give_ref) = refs[:-2], refs[-2:]
    wide = 0
    y_lo = at_ref[3]
    for m in range(2):
        for ref, which in ((keep_ref, y_lo), (give_ref, 1 - y_lo)):
            src = pl.ds(pl.multiple_of(wide + m * HALF + which * 128, 128), 128)
            total = parts[0][:, src].astype(jnp.float32)
            for part in parts[1:]:
                total = total + part[:, src].astype(jnp.float32)
            ref[:, m * 128:(m + 1) * 128] = total


def values_kernel(at_ref, *refs):
    out = refs[-1]
    cols = out.shape[1] // GROUP
    for e, ref in enumerate(refs[:-1]):
        src = lax.rem(at_ref[1] + GROUP - e, GROUP) * cols
        out[:, pl.ds(pl.multiple_of(src, 128), cols)] = ref[:, :cols]


def last_kernel(keep_ref, got_ref, dk_ref, dq_ref):
    done = (keep_ref[...] + got_ref[...]).astype(jnp.bfloat16)
    dk_ref[...] = done[:, :128]
    dq_ref[...] = done[:, 128:]


def mixing_kernel(at_ref, *refs):
    out = refs[-1]
    rows = refs[0].shape[0]
    for p in range(GROUP):
        block = refs[0][...]
        for e, ref in enumerate(refs[1:-1], 1):
            src = lax.rem(at_ref[1] + GROUP - e, GROUP)
            block = jnp.where(src == p, ref[...], block)
        out[p * rows:(p + 1) * rows, :] = block


SMEM = pl.BlockSpec(memory_space=pltpu.SMEM)
VMEM = pl.BlockSpec(memory_space=pltpu.VMEM)
ANY = pl.BlockSpec(memory_space=pl.ANY)
F32, B16 = jnp.float32, jnp.bfloat16


def call(body, grid, ins, outs, scratch, args, micros, vmem=40):
    return pl.pallas_call(
        body,
        grid=grid,
        in_specs=ins,
        out_specs=[spec for spec, _, _ in outs],
        out_shape=[jax.ShapeDtypeStruct(shape, kind) for _, shape, kind in outs],
        scratch_shapes=scratch,
        compiler_params=pltpu.CompilerParams(vmem_limit_bytes=vmem * 2**20),
        cost_estimate=pl.CostEstimate(
            flops=int(micros * 1e9), bytes_accessed=1_000_000, transcendentals=0),
    )(*args)


def fixed(shape, *at):
    return pl.BlockSpec(shape, lambda h: at or (0,) * len(shape))


def by_head(rows, base=0):
    return pl.BlockSpec((rows, 128), lambda h: (0, base + h))


def head_first(*shape):
    return pl.BlockSpec((1,) + shape, lambda h: (h,) + (0,) * len(shape))


def per_device(q_shared, k_shared, mixing, values, cotangent):
    tok, width = q_shared.shape
    peers = lax.axis_size("seq")
    scale = 1.0 / math.sqrt(width)
    me = lax.axis_index("seq")
    head_at = lax.axis_index("head")
    heads = mixing.shape[0] // GROUP
    n_v = heads * 128
    span = GROUP * tok
    at = jnp.stack([lax.rem(head_at, 2), lax.rem(me, GROUP), lax.div(me, GROUP), lax.div(head_at, 2),
                    (me >= peers - GROUP).astype(jnp.int32)])

    def to_group(x, by):
        pairs = [(i, (i + GROUP * by) % peers) for i in range(peers)]
        return lax.ppermute(x, "seq", pairs)

    def turn(x, by):
        pairs = [(i, i - i % GROUP + (i + by) % GROUP) for i in range(peers)]
        return lax.ppermute(x, "seq", pairs)

    def turns(parts):
        return [parts[0]] + [turn(part, e) for e, part in enumerate(parts) if e]

    def core_swap(x):
        return lax.ppermute(x, "head", [(0, 1), (1, 0), (2, 3), (3, 2)])

    whole = lambda x: fixed(x.shape)
    wide = n_v + HALF
    ahead_v = to_group(values, 1)
    *own, ahead = call(
        load_kernel, (), [SMEM] + [ANY] * 4,
        [(VMEM, (tok, 2 * wide), B16)] * GROUP + [(VMEM, (tok, HALF), B16)],
        [pltpu.VMEM((tok, width), B16)] * 2 + [pltpu.SemaphoreType.DMA((10,))],
        (at, values, cotangent, k_shared, q_shared), 3, vmem=56)
    ahead = to_group(ahead, 1)
    own = turns(own)
    before = call(split_kernel, (1,), [SMEM, whole(ahead_v), whole(ahead)],
                  [(fixed((tok, wide)), (tok, wide), B16)] * GROUP, [], (at, ahead_v, ahead), 1)
    before = turns(before)
    vk, q_half, c_own, kq = call(
        gather_kernel, (1,), [SMEM] + [whole(own[0])] * GROUP,
        [(fixed((span, wide)), (span, wide), B16), (fixed((span, HALF)), (span, HALF), B16),
         (fixed((span, n_v)), (span, n_v), B16), (fixed((span, 2 * HALF)), (span, 2 * HALF), B16)], [], (at, *own), 1)
    q_next, c_next = to_group(q_half, -1), to_group(c_own, -1)
    kq_other = core_swap(kq)
    kp, mix = call(
        collect_kernel, (1,),
        [SMEM, fixed((GROUP * heads, width))] + [fixed((tok, HALF), 0, 2)] * GROUP,
        [(fixed((span, HALF)), (span, HALF), B16),
         (fixed((heads, 1, width)), (heads, 1, width), F32)],
        [], (at, mixing, *before), 1)
    kp_other = core_swap(kp)

    stats, grad, w, k_all, q_all = call(
        functools.partial(scores_kernel, scale), (heads,),
        [SMEM, head_first(1, width), by_head(span), fixed((span, HALF), 0, 2), by_head(span),
         fixed((span, HALF)), fixed((span, HALF), 0, 0), fixed((span, HALF), 0, 1)]
        + [by_head(tok)] * GROUP + [fixed((span, HALF))] * 2,
        [(head_first(2, span), (heads, 2, span), F32),
         (head_first(2, 768, 256), (heads, 2, 768, 256), B16),
         (head_first(3, 256, 256), (heads, 3, 256, 256), B16),
         (fixed((2 * span, width)), (2 * span, width), B16),
         (fixed((span, width)), (span, width), B16)],
        [pltpu.VMEM((2 * span, width), B16), pltpu.VMEM((span, width), B16),
         pltpu.VMEM((2 * span, 128), B16)],
        (at, mix, vk, vk, c_own, q_half, kq_other, kq_other, *before, kp, kp_other), 1)
    next_stats = to_group(stats, -1)
    q_next, stats = lax.optimization_barrier((q_next, stats))
    q_next_other = core_swap(q_next)
    dq_mine, dq_other, dmix = call(
        functools.partial(query_kernel, scale), (heads,),
        [SMEM, head_first(1, width), fixed((2 * span, width)), fixed((span, width)),
         head_first(2, 768, 256)],
        [(fixed((span, HALF)), (span, HALF), F32), (fixed((span, HALF)), (span, HALF), B16),
         (head_first(1, width), (heads, 1, width), F32)],
        [pltpu.VMEM((span, width), F32)],
        (at, mix, k_all, q_all, grad), 0.3)

    def from_peer(x, by):
        return lax.ppermute(x, "seq", [(i, i ^ by) for i in range(peers)])

    def exchange(x, a, b):
        return (x + from_peer(x, a)) + (from_peer(x, b) + from_peer(x, a ^ b))

    dk, dv = call(
        key_kernel, (heads,),
        [head_first(1, width), by_head(span), fixed((span, width)),
         head_first(2, 768, 256), head_first(3, 256, 256)],
        [(fixed((span, width)), (span, width), F32), (by_head(span), (span, n_v), F32)],
        [], (mix, c_own, q_all, grad, w), 0.3)
    dk_mine, dk_other, dv = call(
        functools.partial(next_kernel, scale), (heads,),
        [SMEM, head_first(1, width), by_head(span), fixed((span, HALF), 0, 2),
         fixed((span, HALF), 0, 0), by_head(span), fixed((span, HALF)),
         fixed((span, HALF)), head_first(2, span), fixed((span, width)), by_head(span)],
        [(fixed((span, HALF)), (span, HALF), F32), (fixed((span, HALF)), (span, HALF), B16),
         (by_head(span), (span, n_v), B16)],
        [pltpu.VMEM((span, width), B16), pltpu.VMEM((span, width), B16),
         pltpu.VMEM((span, width), F32)],
        (at, mix, vk, vk, kq_other, c_next, q_next, q_next_other, next_stats, dk, dv), 6)
    dk_other, dq_other, dmix = lax.optimization_barrier((dk_other, dq_other, dmix))
    dmix = exchange(dmix.reshape(heads, width), GROUP, 2 * GROUP)

    dk_got, dq_got = core_swap(dk_other), core_swap(dq_other)
    back = call(
        pack_kernel, (1,), [SMEM, whole(dv), whole(dk_mine), whole(dk_got), whole(dq_mine), whole(dq_got)],
        [(fixed((tok, n_v + 2 * HALF)), (tok, n_v + 2 * HALF), B16)] * GROUP, [],
        (at, dv, dk_mine, dk_got, dq_mine, dq_got), 1)
    back = turns(back)
    keep, give = call(sums_kernel, (1,), [SMEM] + [fixed((tok, 2 * HALF), 0, n_v // (2 * HALF))] * GROUP,
                      [(fixed((tok, HALF)), (tok, HALF), F32)] * 2, [], (at, *back), 1)
    dmix = exchange(dmix, 4 * GROUP, 8 * GROUP)
    got = lax.ppermute(give, "head", [(0, 2), (1, 3), (2, 0), (3, 1)])
    (d_values,) = call(values_kernel, (1,), [SMEM] + [fixed((tok, n_v))] * GROUP,
                       [(fixed((tok, GROUP * n_v)), (tok, GROUP * n_v), B16)], [], (at, *back), 1)
    d_key, d_query = call(last_kernel, (1,), [whole(keep)] * 2,
                          [(fixed((tok, 128)), (tok, 128), B16)] * 2, [], (keep, got), 1)

    dmix = turns([dmix] * GROUP)
    (d_mixing,) = call(mixing_kernel, (1,), [SMEM] + [whole(dmix[0])] * GROUP,
                       [(fixed((GROUP * heads, width)), (GROUP * heads, width), F32)], [], (at, *dmix), 1)
    return d_query, d_key, d_values, d_mixing


def solution(mesh):
    placed = (P("seq", None), P("seq", None), P("head", None), P("seq", "head"), P("seq", "head"))
    return jax.shard_map(
        per_device,
        mesh=mesh,
        in_specs=placed,
        out_specs=(P("seq", "head"), P("seq", "head"), P("seq", "head"), P("head", None)),
        check_vma=False,
    )
```

```python
import functools
import math

import jax
import jax.numpy as jnp
from jax import lax
from jax.experimental import pallas as pl
from jax.experimental.pallas import tpu as pltpu
from jax.sharding import PartitionSpec as P

GROUP = 4
HALF = 256
NEG = -1e30
HEADS_AT_ONCE = 4
LOG2E = 1.4426950408889634

NT = (((1,), (1,)), ((), ()))
NN = (((1,), (0,)), ((), ()))
TN = (((0,), (0,)), ((), ()))


def dot(a, b, dims):
    return lax.dot_general(a, b, dims, preferred_element_type=jnp.float32)


def blocks_of(at_ref):
    core = at_ref[0]
    return core, 2 + core, 1 - core, 3 - core


def rows_from(at_ref, by):
    src = lax.rem(at_ref[1] + GROUP - by, GROUP)
    return pl.ds(pl.multiple_of(src * 128, 128), 128)


def scores_kernel(scale, at_ref, mix_ref, v_ref, km_ref, c_ref, qm_ref, ko_ref, qo_ref,
                  vp0_ref, vp1_ref, vp2_ref, vp3_ref, kpm_ref, kpo_ref,
                  stats_ref, grad_ref, w_ref, k_all, q_all, v_all):
    span = q_all.shape[0]
    tile = span // 2
    half = km_ref.shape[1]

    @pl.when(pl.program_id(0) == 0)
    def _():
        k_all[:span, :half] = kpm_ref[...]
        k_all[:span, half:] = kpo_ref[...]
        k_all[span:, :half] = km_ref[...]
        k_all[span:, half:] = ko_ref[...]
        q_all[:, :half] = qm_ref[...]
        q_all[:, half:] = qo_ref[...]

    for e, ref in enumerate((vp0_ref, vp1_ref, vp2_ref, vp3_ref)):
        v_all[rows_from(at_ref, e), :] = ref[...]
    v_all[span:, :] = v_ref[...]
    is_first = at_ref[2] == 0
    row = lax.broadcasted_iota(jnp.int32, (tile, tile), 0)
    col = lax.broadcasted_iota(jnp.int32, (tile, tile), 1)
    for t, j in [(t, j) for t in (0, 1) for j in range(mix_ref.shape[0])]:
        lo = t * tile
        cols = slice(j * 128, (j + 1) * 128)
        mq = (q_all[lo:lo + tile, :].astype(jnp.float32) * mix_ref[j]).astype(jnp.bfloat16)
        up = c_ref[lo:lo + tile, cols]
        s = dot(k_all[lo:lo + 3 * tile, :], mq, NT) * (scale * LOG2E)
        d = dot(v_all[lo:lo + 3 * tile, cols], up, NT)
        s0 = jnp.where((row > col) & jnp.logical_not(is_first), s[:tile], NEG)
        s1 = s[tile:2 * tile]
        if t == 0:
            s1 = jnp.where(is_first, NEG, s1)
        s2 = jnp.where(row <= col, s[2 * tile:], NEG)
        top = jnp.max(jnp.maximum(jnp.maximum(s0, s1), s2), 0, keepdims=True)
        p = [jnp.exp2(part - top) for part in (s0, s1, s2)]
        total = jnp.sum(p[0] + p[1] + p[2], 0, keepdims=True)
        inv = 1.0 / total
        ds = [d[:tile], d[tile:2 * tile], d[2 * tile:]]
        delta = jnp.sum(p[0] * ds[0] + p[1] * ds[1] + p[2] * ds[2], 0, keepdims=True) * inv
        stats_ref[j, 0:1, lo:lo + tile] = top + jnp.log2(total)
        stats_ref[j, 1:2, lo:lo + tile] = delta
        for i in range(3):
            w = p[i] * inv
            grad_ref[j, t, i * tile:(i + 1) * tile, :] = (w * (ds[i] - delta)).astype(jnp.bfloat16)
            if i == 2:
                w_ref[j, 2 * t, :, :] = w.astype(jnp.bfloat16)
            if i == 1 and t == 1:
                w_ref[j, 1, :, :] = w.astype(jnp.bfloat16)


def query_kernel(scale, at_ref, mix_ref, k_ref, q_ref, grad_ref, dqm_ref, dqo_ref, dmix_ref, dq_acc):
    span, width = q_ref.shape
    tile = span // 2
    many = mix_ref.shape[0]

    @pl.when(pl.program_id(0) == 0)
    def _():
        dq_acc[...] = jnp.zeros_like(dq_acc)

    dmix = [jnp.zeros((1, width), jnp.float32) for _ in range(many)]
    for t in (0, 1):
        lo = t * tile
        q_f32 = q_ref[lo:lo + tile, :].astype(jnp.float32)
        dq = 0.0
        for j in range(many):
            qg = dot(grad_ref[j, t], k_ref[lo:lo + 3 * tile, :], TN) * scale
            dq = dq + qg * mix_ref[j]
            dmix[j] = dmix[j] + jnp.sum(qg * q_f32, 0, keepdims=True)
        dq_acc[lo:lo + tile, :] += dq
    for j in range(many):
        for m, block in enumerate(blocks_of(at_ref)):
            dst = pl.ds(pl.multiple_of(block * 128, 128), 128)
            dmix_ref[j, :, dst] = dmix[j][:, m * 128:(m + 1) * 128]

    @pl.when(pl.program_id(0) == pl.num_programs(0) - 1)
    def _():
        dqm_ref[...] = dq_acc[:, :width // 2]
        dqo_ref[...] = dq_acc[:, width // 2:].astype(jnp.bfloat16)


def key_kernel(mix_ref, c_ref, q_ref, grad_ref, w_ref, dk_ref, dv_ref):
    span = q_ref.shape[0]
    tile = span // 2

    @pl.when(pl.program_id(0) == 0)
    def _():
        dk_ref[...] = jnp.zeros_like(dk_ref)

    for j in range(mix_ref.shape[0]):
        cols = slice(j * 128, (j + 1) * 128)
        mq = (q_ref[...].astype(jnp.float32) * mix_ref[j]).astype(jnp.bfloat16)
        dk_ref[...] += dot(grad_ref[j, 1, tile:, :], mq[tile:], NN)
        dk_ref[:tile, :] += dot(grad_ref[j, 0, 2 * tile:, :], mq[:tile], NN)
        dv_ref[tile:, cols] = dot(w_ref[j, 2], c_ref[tile:, cols], NN)
        dv_ref[:tile, cols] = dot(w_ref[j, 1], c_ref[tile:, cols], NN) + dot(w_ref[j, 0], c_ref[:tile, cols], NN)


def next_kernel(scale, at_ref, mix_ref, v_ref, km_ref, ko_ref, cn_ref, qnm_ref, qno_ref, stats_ref,
                dk_ref, dv_ref, dkm_ref, dko_ref, dvo_ref, k_all, q_all, dk_acc):
    span = q_all.shape[0]
    tile = span // 2
    half = km_ref.shape[1]

    @pl.when(pl.program_id(0) == 0)
    def _():
        k_all[:, :half] = km_ref[...]
        k_all[:, half:] = ko_ref[...]
        q_all[:, :half] = qnm_ref[...]
        q_all[:, half:] = qno_ref[...]
        dk_acc[...] = dk_ref[...]

    row = lax.broadcasted_iota(jnp.int32, (tile, tile), 0)
    col = lax.broadcasted_iota(jnp.int32, (tile, tile), 1)
    is_last = at_ref[4] == 1
    seen = (row > col) & jnp.logical_not(is_last)
    for j in range(mix_ref.shape[0]):
        cols = slice(j * 128, (j + 1) * 128)
        dv = [dv_ref[:tile, cols], dv_ref[tile:, cols]]
        for t in (0, 1):
            lo = t * tile
            mq = (q_all[lo:lo + tile, :].astype(jnp.float32) * mix_ref[j]).astype(jnp.bfloat16)
            up = cn_ref[lo:lo + tile, cols]
            lse = stats_ref[j, 0:1, lo:lo + tile]
            delta = stats_ref[j, 1:2, lo:lo + tile]
            s = dot(k_all[lo:, :], mq, NT) * (scale * LOG2E)
            d = dot(v_ref[lo:, cols], up, NT)
            w = jnp.exp2(jnp.where(seen, s[:tile] - lse, NEG))
            if t == 0:
                w = jnp.concatenate([w, jnp.exp2(jnp.where(is_last, NEG, s[tile:] - lse))], 0)
            grad = (w * (d - delta)).astype(jnp.bfloat16)
            add = dot(w.astype(jnp.bfloat16), up, NN)
            if t == 0:
                dv = [dv[0] + add[:tile], dv[1] + add[tile:]]
            else:
                dv[1] = dv[1] + add
            dk_acc[lo:, :] += dot(grad, mq, NN)
        dvo_ref[:tile, cols] = dv[0].astype(jnp.bfloat16)
        dvo_ref[tile:, cols] = dv[1].astype(jnp.bfloat16)

    @pl.when(pl.program_id(0) == pl.num_programs(0) - 1)
    def _():
        dkm_ref[...] = dk_acc[:, :half] * scale
        dko_ref[...] = (dk_acc[:, half:] * scale).astype(jnp.bfloat16)


def load_kernel(at_ref, v_ref, c_ref, k_ref, q_ref, own0_ref, own1_ref, own2_ref, own3_ref,
                ahead_ref, k_in, q_in, sems):
    core, place = at_ref[0], at_ref[1]
    wide = v_ref.shape[1]
    cols = wide // GROUP
    pending = []

    def send(src, dst):
        copy = pltpu.make_async_copy(src, dst, sems.at[len(pending)])
        copy.start()
        pending.append(copy)
        return copy

    shared = [send(k_ref, k_in), send(q_ref, q_in)]
    owns = (own0_ref, own1_ref, own2_ref, own3_ref)
    for e, own in enumerate(owns):
        src = pl.ds(pl.multiple_of(lax.rem(place + e, GROUP) * cols, 128), cols)
        send(v_ref.at[:, src], own.at[:, :cols])
        send(c_ref.at[:, src], own.at[:, cols + 2 * HALF:])
    for copy in shared:
        copy.wait()
    for m in range(2):
        src = pl.ds(pl.multiple_of((2 * m + core) * 128, 128), 128)
        k_block, q_block = k_in[:, src], q_in[:, src]
        ahead_ref[:, m * 128:(m + 1) * 128] = k_block
        for own in owns:
            own[:, cols + m * 128:cols + (m + 1) * 128] = k_block
            own[:, cols + HALF + m * 128:cols + HALF + (m + 1) * 128] = q_block
    for copy in pending[2:]:
        copy.wait()


def split_kernel(at_ref, raw_ref, k_ref, *hops):
    cols = hops[0].shape[1] - HALF
    for e, hop in enumerate(hops):
        src = lax.rem(at_ref[1] + e, GROUP) * cols
        hop[:, :cols] = raw_ref[:, pl.ds(pl.multiple_of(src, 128), cols)]
        hop[:, cols:] = k_ref[...]


def gather_kernel(at_ref, p0_ref, p1_ref, p2_ref, p3_ref, vk_ref, cq_ref, kq_ref):
    half = vk_ref.shape[1]
    for e, ref in enumerate((p0_ref, p1_ref, p2_ref, p3_ref)):
        rows = rows_from(at_ref, e)
        vk_ref[rows, :] = ref[:, :half]
        cq_ref[rows, :half - HALF] = ref[:, half + HALF:]
        cq_ref[rows, half - HALF:] = ref[:, half:half + HALF]
        kq_ref[rows, :] = ref[:, half - HALF:half + HALF]


def collect_kernel(at_ref, mixing_ref, k0_ref, k1_ref, k2_ref, k3_ref, k_ref, mix_ref):
    core, place = at_ref[0], at_ref[1]
    for e, ref in enumerate((k0_ref, k1_ref, k2_ref, k3_ref)):
        k_ref[rows_from(at_ref, e), :] = ref[...]
    for h in range(mix_ref.shape[0]):
        row = mixing_ref[pl.ds(place * mix_ref.shape[0] + h, 1), :]
        blocks = [row[:, i * 128:(i + 1) * 128] for i in range(4)]
        for m, (even, odd) in enumerate(((0, 1), (2, 3), (1, 0), (3, 2))):
            mix_ref[h, :, m * 128:(m + 1) * 128] = jnp.where(core == 0, blocks[even], blocks[odd])


def pack_kernel(at_ref, dv_ref, dk_ref, dk_got_ref, dq_ref, dq_got_ref, *outs):
    cols = dv_ref.shape[1]
    for e, out in enumerate(outs):
        dest = lax.rem(at_ref[1] + e, GROUP)
        rows = pl.ds(pl.multiple_of(dest * 128, 128), 128)
        out[:, :cols] = dv_ref[rows, :]
        dk = dk_ref[rows, :] + dk_got_ref[rows, :].astype(jnp.float32)
        dq = dq_ref[rows, :] + dq_got_ref[rows, :].astype(jnp.float32)
        out[:, cols:cols + HALF] = dk.astype(jnp.bfloat16)
        out[:, cols + HALF:] = dq.astype(jnp.bfloat16)


def sums_kernel(at_ref, *refs):
    parts, (keep_ref, give_ref) = refs[:-2], refs[-2:]
    wide = 0
    y_lo = at_ref[3]
    for m in range(2):
        for ref, which in ((keep_ref, y_lo), (give_ref, 1 - y_lo)):
            src = pl.ds(pl.multiple_of(wide + m * HALF + which * 128, 128), 128)
            total = parts[0][:, src].astype(jnp.float32)
            for part in parts[1:]:
                total = total + part[:, src].astype(jnp.float32)
            ref[:, m * 128:(m + 1) * 128] = total


def values_kernel(at_ref, *refs):
    out = refs[-1]
    cols = out.shape[1] // GROUP
    for e, ref in enumerate(refs[:-1]):
        src = lax.rem(at_ref[1] + GROUP - e, GROUP) * cols
        out[:, pl.ds(pl.multiple_of(src, 128), cols)] = ref[:, :cols]


def last_kernel(keep_ref, got_ref, dk_ref, dq_ref):
    done = (keep_ref[...] + got_ref[...]).astype(jnp.bfloat16)
    dk_ref[...] = done[:, :128]
    dq_ref[...] = done[:, 128:]


def mixing_kernel(at_ref, *refs):
    out = refs[-1]
    rows = refs[0].shape[0]
    for p in range(GROUP):
        block = refs[0][...]
        for e, ref in enumerate(refs[1:-1], 1):
            src = lax.rem(at_ref[1] + GROUP - e, GROUP)
            block = jnp.where(src == p, ref[...], block)
        out[p * rows:(p + 1) * rows, :] = block


SMEM = pl.BlockSpec(memory_space=pltpu.SMEM)
VMEM = pl.BlockSpec(memory_space=pltpu.VMEM)
ANY = pl.BlockSpec(memory_space=pl.ANY)
F32, B16 = jnp.float32, jnp.bfloat16


def call(body, grid, ins, outs, scratch, args, micros, vmem=40):
    return pl.pallas_call(
        body,
        grid=grid,
        in_specs=ins,
        out_specs=[spec for spec, _, _ in outs],
        out_shape=[jax.ShapeDtypeStruct(shape, kind) for _, shape, kind in outs],
        scratch_shapes=scratch,
        compiler_params=pltpu.CompilerParams(vmem_limit_bytes=vmem * 2**20),
        cost_estimate=pl.CostEstimate(
            flops=int(micros * 1e9), bytes_accessed=1_000_000, transcendentals=0),
    )(*args)


def fixed(shape, *at):
    return pl.BlockSpec(shape, lambda h: at or (0,) * len(shape))


def by_head(rows):
    return pl.BlockSpec((rows, 128 * HEADS_AT_ONCE), lambda h: (0, h))


def head_first(*shape):
    return pl.BlockSpec((HEADS_AT_ONCE,) + shape, lambda h: (h,) + (0,) * len(shape))


def per_device(q_shared, k_shared, mixing, values, cotangent):
    tok, width = q_shared.shape
    peers = lax.axis_size("seq")
    scale = 1.0 / math.sqrt(width)
    me = lax.axis_index("seq")
    head_at = lax.axis_index("head")
    heads = mixing.shape[0] // GROUP
    n_v = heads * 128
    span = GROUP * tok
    at = jnp.stack([lax.rem(head_at, 2), lax.rem(me, GROUP), lax.div(me, GROUP), lax.div(head_at, 2),
                    (me >= peers - GROUP).astype(jnp.int32)])

    def to_group(x, by):
        pairs = [(i, (i + GROUP * by) % peers) for i in range(peers)]
        return lax.ppermute(x, "seq", pairs)

    def turn(x, by):
        pairs = [(i, i - i % GROUP + (i + by) % GROUP) for i in range(peers)]
        return lax.ppermute(x, "seq", pairs)

    def turns(parts):
        return [parts[0]] + [turn(part, e) for e, part in enumerate(parts) if e]

    def core_swap(x):
        return lax.ppermute(x, "head", [(0, 1), (1, 0), (2, 3), (3, 2)])

    whole = lambda x: fixed(x.shape)
    wide = n_v + HALF
    ahead_v = to_group(values, 1)
    *own, ahead = call(
        load_kernel, (), [SMEM] + [ANY] * 4,
        [(VMEM, (tok, 2 * wide), B16)] * GROUP + [(VMEM, (tok, HALF), B16)],
        [pltpu.VMEM((tok, width), B16)] * 2 + [pltpu.SemaphoreType.DMA((10,))],
        (at, values, cotangent, k_shared, q_shared), 3, vmem=56)
    ahead = to_group(ahead, 1)
    own = turns(own)
    before = call(split_kernel, (1,), [SMEM, whole(ahead_v), whole(ahead)],
                  [(fixed((tok, wide)), (tok, wide), B16)] * GROUP, [], (at, ahead_v, ahead), 1)
    before = turns(before)
    vk, cq, kq = call(
        gather_kernel, (1,), [SMEM] + [whole(own[0])] * GROUP,
        [(fixed((span, wide)), (span, wide), B16)] * 2
        + [(fixed((span, 2 * HALF)), (span, 2 * HALF), B16)], [], (at, *own), 1)
    cq_next = to_group(cq, -1)
    kq_other = core_swap(kq)
    kp, mix = call(
        collect_kernel, (1,),
        [SMEM, fixed((GROUP * heads, width))] + [fixed((tok, HALF), 0, 2)] * GROUP,
        [(fixed((span, HALF)), (span, HALF), B16),
         (fixed((heads, 1, width)), (heads, 1, width), F32)],
        [], (at, mixing, *before), 1)
    kp_other = core_swap(kp)

    stats, grad, w, k_all, q_all = call(
        functools.partial(scores_kernel, scale), (heads // HEADS_AT_ONCE,),
        [SMEM, head_first(1, width), by_head(span), fixed((span, HALF), 0, 2), by_head(span),
         fixed((span, HALF), 0, n_v // HALF), fixed((span, HALF), 0, 0), fixed((span, HALF), 0, 1)]
        + [by_head(tok)] * GROUP + [fixed((span, HALF))] * 2,
        [(head_first(2, span), (heads, 2, span), F32),
         (head_first(2, 768, 256), (heads, 2, 768, 256), B16),
         (head_first(3, 256, 256), (heads, 3, 256, 256), B16),
         (fixed((2 * span, width)), (2 * span, width), B16),
         (fixed((span, width)), (span, width), B16)],
        [pltpu.VMEM((2 * span, 128 * HEADS_AT_ONCE), B16)],
        (at, mix, vk, vk, cq, cq, kq_other, kq_other, *before, kp, kp_other), 2.5)
    next_stats = to_group(stats, -1)
    dq_mine, dq_other, dmix = call(
        functools.partial(query_kernel, scale), (heads // HEADS_AT_ONCE,),
        [SMEM, head_first(1, width), fixed((2 * span, width)), fixed((span, width)),
         head_first(2, 768, 256)],
        [(fixed((span, HALF)), (span, HALF), F32), (fixed((span, HALF)), (span, HALF), B16),
         (head_first(1, width), (heads, 1, width), F32)],
        [pltpu.VMEM((span, width), F32)],
        (at, mix, k_all, q_all, grad), 0.3)

    def from_peer(x, by):
        return lax.ppermute(x, "seq", [(i, i ^ by) for i in range(peers)])

    def exchange(x, a, b):
        return (x + from_peer(x, a)) + (from_peer(x, b) + from_peer(x, a ^ b))

    dk, dv = call(
        key_kernel, (heads // HEADS_AT_ONCE,),
        [head_first(1, width), by_head(span), fixed((span, width)),
         head_first(2, 768, 256), head_first(3, 256, 256)],
        [(fixed((span, width)), (span, width), F32), (by_head(span), (span, n_v), F32)],
        [], (mix, cq, q_all, grad, w), 0.3)
    cq_next, next_stats, dk, dq_mine = lax.optimization_barrier((cq_next, next_stats, dk, dq_mine))
    q_next_other = core_swap(cq_next[:, n_v:])
    dk_mine, dk_other, dv = call(
        functools.partial(next_kernel, scale), (heads // HEADS_AT_ONCE,),
        [SMEM, head_first(1, width), by_head(span), fixed((span, HALF), 0, 2),
         fixed((span, HALF), 0, 0), by_head(span), fixed((span, HALF), 0, n_v // HALF),
         fixed((span, HALF)), head_first(2, span), fixed((span, width)), by_head(span)],
        [(fixed((span, HALF)), (span, HALF), F32), (fixed((span, HALF)), (span, HALF), B16),
         (by_head(span), (span, n_v), B16)],
        [pltpu.VMEM((span, width), B16), pltpu.VMEM((span, width), B16),
         pltpu.VMEM((span, width), F32)],
        (at, mix, vk, vk, kq_other, cq_next, cq_next, q_next_other, next_stats, dk, dv), 6)
    dk_other, dq_other, dmix = lax.optimization_barrier((dk_other, dq_other, dmix))
    dmix = exchange(dmix.reshape(heads, width), GROUP, 2 * GROUP)

    dk_got, dq_got = core_swap(dk_other), core_swap(dq_other)
    back = call(
        pack_kernel, (1,), [SMEM, whole(dv), whole(dk_mine), whole(dk_got), whole(dq_mine), whole(dq_got)],
        [(fixed((tok, n_v + 2 * HALF)), (tok, n_v + 2 * HALF), B16)] * GROUP, [],
        (at, dv, dk_mine, dk_got, dq_mine, dq_got), 1)
    back = turns(back)
    keep, give = call(sums_kernel, (1,), [SMEM] + [fixed((tok, 2 * HALF), 0, n_v // (2 * HALF))] * GROUP,
                      [(fixed((tok, HALF)), (tok, HALF), F32)] * 2, [], (at, *back), 1)
    dmix = exchange(dmix, 4 * GROUP, 8 * GROUP)
    got = lax.ppermute(give, "head", [(0, 2), (1, 3), (2, 0), (3, 1)])
    (d_values,) = call(values_kernel, (1,), [SMEM] + [fixed((tok, n_v))] * GROUP,
                       [(fixed((tok, GROUP * n_v)), (tok, GROUP * n_v), B16)], [], (at, *back), 1)
    d_key, d_query = call(last_kernel, (1,), [whole(keep)] * 2,
                          [(fixed((tok, 128)), (tok, 128), B16)] * 2, [], (keep, got), 1)

    dmix = turns([dmix] * GROUP)
    (d_mixing,) = call(mixing_kernel, (1,), [SMEM] + [whole(dmix[0])] * GROUP,
                       [(fixed((GROUP * heads, width)), (GROUP * heads, width), F32)], [], (at, *dmix), 1)
    return d_query, d_key, d_values, d_mixing


def solution(mesh):
    placed = (P("seq", None), P("seq", None), P("head", None), P("seq", "head"), P("seq", "head"))
    return jax.shard_map(
        per_device,
        mesh=mesh,
        in_specs=placed,
        out_specs=(P("seq", "head"), P("seq", "head"), P("seq", "head"), P("head", None)),
        check_vma=False,
    )
```

```python
import functools
import math

import jax
import jax.numpy as jnp
from jax import lax
from jax.experimental import pallas as pl
from jax.experimental.pallas import tpu as pltpu
from jax.sharding import PartitionSpec as P

GROUP = 4
HALF = 256
NEG = -1e30
HEADS_AT_ONCE = 4
LOG2E = 1.4426950408889634

NT = (((1,), (1,)), ((), ()))
NN = (((1,), (0,)), ((), ()))
TN = (((0,), (0,)), ((), ()))


def dot(a, b, dims):
    return lax.dot_general(a, b, dims, preferred_element_type=jnp.float32)


def blocks_of(at_ref):
    core = at_ref[0]
    return core, 2 + core, 1 - core, 3 - core


def rows_from(at_ref, by):
    src = lax.rem(at_ref[1] + GROUP - by, GROUP)
    return pl.ds(pl.multiple_of(src * 128, 128), 128)


def scores_kernel(scale, at_ref, mix_ref, v_ref, km_ref, c_ref, qm_ref, ko_ref, qo_ref,
                  vp0_ref, vp1_ref, vp2_ref, vp3_ref, kpm_ref, kpo_ref,
                  stats_ref, grad_ref, w_ref, k_all, q_all, v_all):
    span = q_all.shape[0]
    tile = span // 2
    half = km_ref.shape[1]

    @pl.when(pl.program_id(0) == 0)
    def _():
        k_all[:span, :half] = kpm_ref[...]
        k_all[:span, half:] = kpo_ref[...]
        k_all[span:, :half] = km_ref[...]
        k_all[span:, half:] = ko_ref[...]
        q_all[:, :half] = qm_ref[...]
        q_all[:, half:] = qo_ref[...]

    for e, ref in enumerate((vp0_ref, vp1_ref, vp2_ref, vp3_ref)):
        v_all[rows_from(at_ref, e), :] = ref[...]
    v_all[span:, :] = v_ref[...]
    is_first = at_ref[2] == 0
    row = lax.broadcasted_iota(jnp.int32, (tile, tile), 0)
    col = lax.broadcasted_iota(jnp.int32, (tile, tile), 1)
    for t, j in [(t, j) for t in (0, 1) for j in range(mix_ref.shape[0])]:
        lo = t * tile
        cols = slice(j * 128, (j + 1) * 128)
        mq = (q_all[lo:lo + tile, :].astype(jnp.float32) * mix_ref[j]).astype(jnp.bfloat16)
        up = c_ref[lo:lo + tile, cols]
        s = dot(k_all[lo:lo + 3 * tile, :], mq, NT) * (scale * LOG2E)
        d = dot(v_all[lo:lo + 3 * tile, cols], up, NT)
        s0 = jnp.where((row > col) & jnp.logical_not(is_first), s[:tile], NEG)
        s1 = s[tile:2 * tile]
        if t == 0:
            s1 = jnp.where(is_first, NEG, s1)
        s2 = jnp.where(row <= col, s[2 * tile:], NEG)
        top = jnp.max(jnp.maximum(jnp.maximum(s0, s1), s2), 0, keepdims=True)
        p = [jnp.exp2(part - top) for part in (s0, s1, s2)]
        total = jnp.sum(p[0] + p[1] + p[2], 0, keepdims=True)
        inv = 1.0 / total
        ds = [d[:tile], d[tile:2 * tile], d[2 * tile:]]
        delta = jnp.sum(p[0] * ds[0] + p[1] * ds[1] + p[2] * ds[2], 0, keepdims=True) * inv
        stats_ref[j, 0:1, lo:lo + tile] = top + jnp.log2(total)
        stats_ref[j, 1:2, lo:lo + tile] = delta
        for i in range(3):
            w = p[i] * inv
            grad_ref[j, t, i * tile:(i + 1) * tile, :] = (w * (ds[i] - delta)).astype(jnp.bfloat16)
            if i == 2:
                w_ref[j, 2 * t, :, :] = w.astype(jnp.bfloat16)
            if i == 1 and t == 1:
                w_ref[j, 1, :, :] = w.astype(jnp.bfloat16)


def query_kernel(scale, at_ref, mix_ref, k_ref, q_ref, grad_ref, dqm_ref, dqo_ref, dmix_ref, dq_acc):
    span, width = q_ref.shape
    tile = span // 2
    many = mix_ref.shape[0]

    @pl.when(pl.program_id(0) == 0)
    def _():
        dq_acc[...] = jnp.zeros_like(dq_acc)

    dmix = [jnp.zeros((1, width), jnp.float32) for _ in range(many)]
    for t in (0, 1):
        lo = t * tile
        q_f32 = q_ref[lo:lo + tile, :].astype(jnp.float32)
        dq = 0.0
        for j in range(many):
            qg = dot(grad_ref[j, t], k_ref[lo:lo + 3 * tile, :], TN) * scale
            dq = dq + qg * mix_ref[j]
            dmix[j] = dmix[j] + jnp.sum(qg * q_f32, 0, keepdims=True)
        dq_acc[lo:lo + tile, :] += dq
    for j in range(many):
        for m, block in enumerate(blocks_of(at_ref)):
            dst = pl.ds(pl.multiple_of(block * 128, 128), 128)
            dmix_ref[j, :, dst] = dmix[j][:, m * 128:(m + 1) * 128]

    @pl.when(pl.program_id(0) == pl.num_programs(0) - 1)
    def _():
        dqm_ref[...] = dq_acc[:, :width // 2]
        dqo_ref[...] = dq_acc[:, width // 2:].astype(jnp.bfloat16)


def key_kernel(mix_ref, c_ref, q_ref, grad_ref, w_ref, dk_ref, dv_ref):
    span = q_ref.shape[0]
    tile = span // 2

    @pl.when(pl.program_id(0) == 0)
    def _():
        dk_ref[...] = jnp.zeros_like(dk_ref)

    for j in range(mix_ref.shape[0]):
        cols = slice(j * 128, (j + 1) * 128)
        mq = (q_ref[...].astype(jnp.float32) * mix_ref[j]).astype(jnp.bfloat16)
        dk_ref[...] += dot(grad_ref[j, 1, tile:, :], mq[tile:], NN)
        dk_ref[:tile, :] += dot(grad_ref[j, 0, 2 * tile:, :], mq[:tile], NN)
        dv_ref[tile:, cols] = dot(w_ref[j, 2], c_ref[tile:, cols], NN)
        dv_ref[:tile, cols] = dot(w_ref[j, 1], c_ref[tile:, cols], NN) + dot(w_ref[j, 0], c_ref[:tile, cols], NN)


def next_kernel(scale, at_ref, mix_ref, v_ref, km_ref, ko_ref, cn_ref, qnm_ref, qno_ref, stats_ref,
                dk_ref, dv_ref, dkm_ref, dko_ref, dvo_ref, k_all, q_all, dk_acc):
    span = q_all.shape[0]
    tile = span // 2
    half = km_ref.shape[1]

    @pl.when(pl.program_id(0) == 0)
    def _():
        k_all[:, :half] = km_ref[...]
        k_all[:, half:] = ko_ref[...]
        q_all[:, :half] = qnm_ref[...]
        q_all[:, half:] = qno_ref[...]
        dk_acc[...] = dk_ref[...]

    row = lax.broadcasted_iota(jnp.int32, (tile, tile), 0)
    col = lax.broadcasted_iota(jnp.int32, (tile, tile), 1)
    is_last = at_ref[4] == 1
    seen = (row > col) & jnp.logical_not(is_last)
    for j in range(mix_ref.shape[0]):
        cols = slice(j * 128, (j + 1) * 128)
        dv = [dv_ref[:tile, cols], dv_ref[tile:, cols]]
        for t in (0, 1):
            lo = t * tile
            mq = (q_all[lo:lo + tile, :].astype(jnp.float32) * mix_ref[j]).astype(jnp.bfloat16)
            up = cn_ref[lo:lo + tile, cols]
            lse = stats_ref[j, 0:1, lo:lo + tile]
            delta = stats_ref[j, 1:2, lo:lo + tile]
            s = dot(k_all[lo:, :], mq, NT) * (scale * LOG2E)
            d = dot(v_ref[lo:, cols], up, NT)
            w = jnp.exp2(jnp.where(seen, s[:tile] - lse, NEG))
            if t == 0:
                w = jnp.concatenate([w, jnp.exp2(jnp.where(is_last, NEG, s[tile:] - lse))], 0)
            grad = (w * (d - delta)).astype(jnp.bfloat16)
            add = dot(w.astype(jnp.bfloat16), up, NN)
            if t == 0:
                dv = [dv[0] + add[:tile], dv[1] + add[tile:]]
            else:
                dv[1] = dv[1] + add
            dk_acc[lo:, :] += dot(grad, mq, NN)
        dvo_ref[:tile, cols] = dv[0].astype(jnp.bfloat16)
        dvo_ref[tile:, cols] = dv[1].astype(jnp.bfloat16)

    @pl.when(pl.program_id(0) == pl.num_programs(0) - 1)
    def _():
        dkm_ref[...] = dk_acc[:, :half] * scale
        dko_ref[...] = (dk_acc[:, half:] * scale).astype(jnp.bfloat16)


def load_kernel(v_ref, c_ref, k_ref, q_ref, own0_ref, own1_ref, own2_ref, own3_ref,
                ahead_ref, k_in, q_in, sems):
    core, place = lax.rem(lax.axis_index("head"), 2), lax.rem(lax.axis_index("seq"), GROUP)
    wide = v_ref.shape[1]
    cols = wide // GROUP
    pending = []

    def send(src, dst):
        copy = pltpu.make_async_copy(src, dst, sems.at[len(pending)])
        copy.start()
        pending.append(copy)
        return copy

    shared = [send(k_ref, k_in), send(q_ref, q_in)]
    owns = (own0_ref, own1_ref, own2_ref, own3_ref)
    for e, own in enumerate(owns):
        src = pl.ds(pl.multiple_of(lax.rem(place + e, GROUP) * cols, 128), cols)
        send(v_ref.at[:, src], own.at[:, :cols])
        send(c_ref.at[:, src], own.at[:, cols + 2 * HALF:])
    for copy in shared:
        copy.wait()
    for m in range(2):
        src = pl.ds(pl.multiple_of((2 * m + core) * 128, 128), 128)
        k_block, q_block = k_in[:, src], q_in[:, src]
        ahead_ref[:, m * 128:(m + 1) * 128] = k_block
        for own in owns:
            own[:, cols + m * 128:cols + (m + 1) * 128] = k_block
            own[:, cols + HALF + m * 128:cols + HALF + (m + 1) * 128] = q_block
    for copy in pending[2:]:
        copy.wait()


def split_kernel(at_ref, raw_ref, k_ref, *hops):
    cols = hops[0].shape[1] - HALF
    for e, hop in enumerate(hops):
        src = lax.rem(at_ref[1] + e, GROUP) * cols
        hop[:, :cols] = raw_ref[:, pl.ds(pl.multiple_of(src, 128), cols)]
        hop[:, cols:] = k_ref[...]


def gather_kernel(at_ref, p0_ref, p1_ref, p2_ref, p3_ref, vk_ref, cq_ref, kq_ref):
    half = vk_ref.shape[1]
    for e, ref in enumerate((p0_ref, p1_ref, p2_ref, p3_ref)):
        rows = rows_from(at_ref, e)
        vk_ref[rows, :] = ref[:, :half]
        cq_ref[rows, :half - HALF] = ref[:, half + HALF:]
        cq_ref[rows, half - HALF:] = ref[:, half:half + HALF]
        kq_ref[rows, :] = ref[:, half - HALF:half + HALF]


def collect_kernel(at_ref, mixing_ref, k0_ref, k1_ref, k2_ref, k3_ref, k_ref, mix_ref):
    core, place = at_ref[0], at_ref[1]
    for e, ref in enumerate((k0_ref, k1_ref, k2_ref, k3_ref)):
        k_ref[rows_from(at_ref, e), :] = ref[...]
    for h in range(mix_ref.shape[0]):
        row = mixing_ref[pl.ds(place * mix_ref.shape[0] + h, 1), :]
        blocks = [row[:, i * 128:(i + 1) * 128] for i in range(4)]
        for m, (even, odd) in enumerate(((0, 1), (2, 3), (1, 0), (3, 2))):
            mix_ref[h, :, m * 128:(m + 1) * 128] = jnp.where(core == 0, blocks[even], blocks[odd])


def pack_kernel(at_ref, dv_ref, dk_ref, dk_got_ref, dq_ref, dq_got_ref, *outs):
    cols = dv_ref.shape[1]
    for e, out in enumerate(outs):
        dest = lax.rem(at_ref[1] + e, GROUP)
        rows = pl.ds(pl.multiple_of(dest * 128, 128), 128)
        out[:, :cols] = dv_ref[rows, :]
        dk = dk_ref[rows, :] + dk_got_ref[rows, :].astype(jnp.float32)
        dq = dq_ref[rows, :] + dq_got_ref[rows, :].astype(jnp.float32)
        out[:, cols:cols + HALF] = dk.astype(jnp.bfloat16)
        out[:, cols + HALF:] = dq.astype(jnp.bfloat16)


def sums_kernel(at_ref, *refs):
    parts, (keep_ref, give_ref) = refs[:-2], refs[-2:]
    wide = 0
    y_lo = at_ref[3]
    for m in range(2):
        for ref, which in ((keep_ref, y_lo), (give_ref, 1 - y_lo)):
            src = pl.ds(pl.multiple_of(wide + m * HALF + which * 128, 128), 128)
            total = parts[0][:, src].astype(jnp.float32)
            for part in parts[1:]:
                total = total + part[:, src].astype(jnp.float32)
            ref[:, m * 128:(m + 1) * 128] = total


def values_kernel(at_ref, *refs):
    out = refs[-1]
    cols = out.shape[1] // GROUP
    for e, ref in enumerate(refs[:-1]):
        src = lax.rem(at_ref[1] + GROUP - e, GROUP) * cols
        out[:, pl.ds(pl.multiple_of(src, 128), cols)] = ref[:, :cols]


def last_kernel(keep_ref, got_ref, dk_ref, dq_ref):
    done = (keep_ref[...] + got_ref[...]).astype(jnp.bfloat16)
    dk_ref[...] = done[:, :128]
    dq_ref[...] = done[:, 128:]


def mixing_kernel(at_ref, *refs):
    out = refs[-1]
    rows = refs[0].shape[0]
    for p in range(GROUP):
        block = refs[0][...]
        for e, ref in enumerate(refs[1:-1], 1):
            src = lax.rem(at_ref[1] + GROUP - e, GROUP)
            block = jnp.where(src == p, ref[...], block)
        out[p * rows:(p + 1) * rows, :] = block


SMEM = pl.BlockSpec(memory_space=pltpu.SMEM)
VMEM = pl.BlockSpec(memory_space=pltpu.VMEM)
ANY = pl.BlockSpec(memory_space=pl.ANY)
F32, B16 = jnp.float32, jnp.bfloat16


def call(body, grid, ins, outs, scratch, args, micros, vmem=40):
    return pl.pallas_call(
        body,
        grid=grid,
        in_specs=ins,
        out_specs=[spec for spec, _, _ in outs],
        out_shape=[jax.ShapeDtypeStruct(shape, kind) for _, shape, kind in outs],
        scratch_shapes=scratch,
        compiler_params=pltpu.CompilerParams(vmem_limit_bytes=vmem * 2**20),
        cost_estimate=pl.CostEstimate(
            flops=int(micros * 1e9), bytes_accessed=1_000_000, transcendentals=0),
    )(*args)


def fixed(shape, *at):
    return pl.BlockSpec(shape, lambda h: at or (0,) * len(shape))


def by_head(rows):
    return pl.BlockSpec((rows, 128 * HEADS_AT_ONCE), lambda h: (0, h))


def head_first(*shape):
    return pl.BlockSpec((HEADS_AT_ONCE,) + shape, lambda h: (h,) + (0,) * len(shape))


def per_device(q_shared, k_shared, mixing, values, cotangent):
    tok, width = q_shared.shape
    peers = lax.axis_size("seq")
    scale = 1.0 / math.sqrt(width)
    me = lax.axis_index("seq")
    head_at = lax.axis_index("head")
    heads = mixing.shape[0] // GROUP
    n_v = heads * 128
    span = GROUP * tok
    at = jnp.stack([lax.rem(head_at, 2), lax.rem(me, GROUP), lax.div(me, GROUP), lax.div(head_at, 2),
                    (me >= peers - GROUP).astype(jnp.int32)])

    def to_group(x, by):
        pairs = [(i, (i + GROUP * by) % peers) for i in range(peers)]
        return lax.ppermute(x, "seq", pairs)

    def turn(x, by):
        pairs = [(i, i - i % GROUP + (i + by) % GROUP) for i in range(peers)]
        return lax.ppermute(x, "seq", pairs)

    def turns(parts):
        return [parts[0]] + [turn(part, e) for e, part in enumerate(parts) if e]

    def core_swap(x):
        return lax.ppermute(x, "head", [(0, 1), (1, 0), (2, 3), (3, 2)])

    whole = lambda x: fixed(x.shape)
    wide = n_v + HALF
    ahead_v = to_group(values, 1)
    *own, ahead = call(
        load_kernel, (), [ANY] * 4,
        [(VMEM, (tok, 2 * wide), B16)] * GROUP + [(VMEM, (tok, HALF), B16)],
        [pltpu.VMEM((tok, width), B16)] * 2 + [pltpu.SemaphoreType.DMA((10,))],
        (values, cotangent, k_shared, q_shared), 3, vmem=56)
    ahead = to_group(ahead, 1)
    own = turns(own)
    before = call(split_kernel, (1,), [SMEM, whole(ahead_v), whole(ahead)],
                  [(fixed((tok, wide)), (tok, wide), B16)] * GROUP, [], (at, ahead_v, ahead), 1)
    before = turns(before)
    vk, cq, kq = call(
        gather_kernel, (1,), [SMEM] + [whole(own[0])] * GROUP,
        [(fixed((span, wide)), (span, wide), B16)] * 2
        + [(fixed((span, 2 * HALF)), (span, 2 * HALF), B16)], [], (at, *own), 1)
    cq_next = to_group(cq, -1)
    kq_other = core_swap(kq)
    kp, mix = call(
        collect_kernel, (1,),
        [SMEM, fixed((GROUP * heads, width))] + [fixed((tok, HALF), 0, 2)] * GROUP,
        [(fixed((span, HALF)), (span, HALF), B16),
         (fixed((heads, 1, width)), (heads, 1, width), F32)],
        [], (at, mixing, *before), 1)
    kp_other = core_swap(kp)

    stats, grad, w, k_all, q_all = call(
        functools.partial(scores_kernel, scale), (heads // HEADS_AT_ONCE,),
        [SMEM, head_first(1, width), by_head(span), fixed((span, HALF), 0, 2), by_head(span),
         fixed((span, HALF), 0, n_v // HALF), fixed((span, HALF), 0, 0), fixed((span, HALF), 0, 1)]
        + [by_head(tok)] * GROUP + [fixed((span, HALF))] * 2,
        [(head_first(2, span), (heads, 2, span), F32),
         (head_first(2, 768, 256), (heads, 2, 768, 256), B16),
         (head_first(3, 256, 256), (heads, 3, 256, 256), B16),
         (fixed((2 * span, width)), (2 * span, width), B16),
         (fixed((span, width)), (span, width), B16)],
        [pltpu.VMEM((2 * span, 128 * HEADS_AT_ONCE), B16)],
        (at, mix, vk, vk, cq, cq, kq_other, kq_other, *before, kp, kp_other), 2.5)
    next_stats = to_group(stats, -1)
    dq_mine, dq_other, dmix = call(
        functools.partial(query_kernel, scale), (heads // HEADS_AT_ONCE,),
        [SMEM, head_first(1, width), fixed((2 * span, width)), fixed((span, width)),
         head_first(2, 768, 256)],
        [(fixed((span, HALF)), (span, HALF), F32), (fixed((span, HALF)), (span, HALF), B16),
         (head_first(1, width), (heads, 1, width), F32)],
        [pltpu.VMEM((span, width), F32)],
        (at, mix, k_all, q_all, grad), 0.3)

    def from_peer(x, by):
        return lax.ppermute(x, "seq", [(i, i ^ by) for i in range(peers)])

    def exchange(x, a, b):
        return (x + from_peer(x, a)) + (from_peer(x, b) + from_peer(x, a ^ b))

    dk, dv = call(
        key_kernel, (heads // HEADS_AT_ONCE,),
        [head_first(1, width), by_head(span), fixed((span, width)),
         head_first(2, 768, 256), head_first(3, 256, 256)],
        [(fixed((span, width)), (span, width), F32), (by_head(span), (span, n_v), F32)],
        [], (mix, cq, q_all, grad, w), 0.3)
    cq_next, next_stats, dk, dq_mine = lax.optimization_barrier((cq_next, next_stats, dk, dq_mine))
    q_next_other = core_swap(cq_next[:, n_v:])
    dk_mine, dk_other, dv = call(
        functools.partial(next_kernel, scale), (heads // HEADS_AT_ONCE,),
        [SMEM, head_first(1, width), by_head(span), fixed((span, HALF), 0, 2),
         fixed((span, HALF), 0, 0), by_head(span), fixed((span, HALF), 0, n_v // HALF),
         fixed((span, HALF)), head_first(2, span), fixed((span, width)), by_head(span)],
        [(fixed((span, HALF)), (span, HALF), F32), (fixed((span, HALF)), (span, HALF), B16),
         (by_head(span), (span, n_v), B16)],
        [pltpu.VMEM((span, width), B16), pltpu.VMEM((span, width), B16),
         pltpu.VMEM((span, width), F32)],
        (at, mix, vk, vk, kq_other, cq_next, cq_next, q_next_other, next_stats, dk, dv), 6)
    dk_other, dmix = lax.optimization_barrier((dk_other, dmix))
    dmix = exchange(dmix.reshape(heads, width), GROUP, 2 * GROUP)

    dk_got, dq_got = core_swap(dk_other), core_swap(dq_other)
    back = call(
        pack_kernel, (1,), [SMEM, whole(dv), whole(dk_mine), whole(dk_got), whole(dq_mine), whole(dq_got)],
        [(fixed((tok, n_v + 2 * HALF)), (tok, n_v + 2 * HALF), B16)] * GROUP, [],
        (at, dv, dk_mine, dk_got, dq_mine, dq_got), 1)
    back = turns(back)
    keep, give = call(sums_kernel, (1,), [SMEM] + [fixed((tok, 2 * HALF), 0, n_v // (2 * HALF))] * GROUP,
                      [(fixed((tok, HALF)), (tok, HALF), F32)] * 2, [], (at, *back), 1)
    dmix = exchange(dmix, 4 * GROUP, 8 * GROUP)
    got = lax.ppermute(give, "head", [(0, 2), (1, 3), (2, 0), (3, 1)])
    (d_values,) = call(values_kernel, (1,), [SMEM] + [fixed((tok, n_v))] * GROUP,
                       [(fixed((tok, GROUP * n_v)), (tok, GROUP * n_v), B16)], [], (at, *back), 1)
    d_key, d_query = call(last_kernel, (1,), [whole(keep)] * 2,
                          [(fixed((tok, 128)), (tok, 128), B16)] * 2, [], (keep, got), 1)

    dmix = turns([dmix] * GROUP)
    (d_mixing,) = call(mixing_kernel, (1,), [SMEM] + [whole(dmix[0])] * GROUP,
                       [(fixed((GROUP * heads, width)), (GROUP * heads, width), F32)], [], (at, *dmix), 1)
    return d_query, d_key, d_values, d_mixing


def solution(mesh):
    placed = (P("seq", None), P("seq", None), P("head", None), P("seq", "head"), P("seq", "head"))
    return jax.shard_map(
        per_device,
        mesh=mesh,
        in_specs=placed,
        out_specs=(P("seq", "head"), P("seq", "head"), P("seq", "head"), P("head", None)),
        check_vma=False,
    )
```

```python
import functools
import math

import jax
import jax.numpy as jnp
from jax import lax
from jax.experimental import pallas as pl
from jax.experimental.pallas import tpu as pltpu
from jax.sharding import PartitionSpec as P

GROUP = 4
HALF = 256
NEG = -1e30
HEADS_AT_ONCE = 4
LOG2E = 1.4426950408889634

NT = (((1,), (1,)), ((), ()))
NN = (((1,), (0,)), ((), ()))
TN = (((0,), (0,)), ((), ()))


def dot(a, b, dims):
    return lax.dot_general(a, b, dims, preferred_element_type=jnp.float32)


def blocks_of(at_ref):
    core = at_ref[0]
    return core, 2 + core, 1 - core, 3 - core


def rows_from(at_ref, by):
    src = lax.rem(at_ref[1] + GROUP - by, GROUP)
    return pl.ds(pl.multiple_of(src * 128, 128), 128)


def scores_kernel(scale, at_ref, mix_ref, v_ref, km_ref, c_ref, qm_ref, ko_ref, qo_ref,
                  vp0_ref, vp1_ref, vp2_ref, vp3_ref, kpm_ref, kpo_ref,
                  stats_ref, grad_ref, w_ref, k_all, q_all, v_all):
    span = q_all.shape[0]
    tile = span // 2
    half = km_ref.shape[1]

    @pl.when(pl.program_id(0) == 0)
    def _():
        k_all[:span, :half] = kpm_ref[...]
        k_all[:span, half:] = kpo_ref[...]
        k_all[span:, :half] = km_ref[...]
        k_all[span:, half:] = ko_ref[...]
        q_all[:, :half] = qm_ref[...]
        q_all[:, half:] = qo_ref[...]

    for e, ref in enumerate((vp0_ref, vp1_ref, vp2_ref, vp3_ref)):
        v_all[rows_from(at_ref, e), :] = ref[...]
    v_all[span:, :] = v_ref[...]
    is_first = at_ref[2] == 0
    row = lax.broadcasted_iota(jnp.int32, (tile, tile), 0)
    col = lax.broadcasted_iota(jnp.int32, (tile, tile), 1)
    for t, j in [(t, j) for t in (0, 1) for j in range(mix_ref.shape[0])]:
        lo = t * tile
        cols = slice(j * 128, (j + 1) * 128)
        mq = (q_all[lo:lo + tile, :].astype(jnp.float32) * mix_ref[j]).astype(jnp.bfloat16)
        up = c_ref[lo:lo + tile, cols]
        s = dot(k_all[lo:lo + 3 * tile, :], mq, NT) * (scale * LOG2E)
        d = dot(v_all[lo:lo + 3 * tile, cols], up, NT)
        s0 = jnp.where((row > col) & jnp.logical_not(is_first), s[:tile], NEG)
        s1 = s[tile:2 * tile]
        if t == 0:
            s1 = jnp.where(is_first, NEG, s1)
        s2 = jnp.where(row <= col, s[2 * tile:], NEG)
        top = jnp.max(jnp.maximum(jnp.maximum(s0, s1), s2), 0, keepdims=True)
        p = [jnp.exp2(part - top) for part in (s0, s1, s2)]
        total = jnp.sum(p[0] + p[1] + p[2], 0, keepdims=True)
        inv = 1.0 / total
        ds = [d[:tile], d[tile:2 * tile], d[2 * tile:]]
        delta = jnp.sum(p[0] * ds[0] + p[1] * ds[1] + p[2] * ds[2], 0, keepdims=True) * inv
        stats_ref[j, 0:1, lo:lo + tile] = top + jnp.log2(total)
        stats_ref[j, 1:2, lo:lo + tile] = delta
        for i in range(3):
            w = p[i] * inv
            grad_ref[j, t, i * tile:(i + 1) * tile, :] = (w * (ds[i] - delta)).astype(jnp.bfloat16)
            if i == 2:
                w_ref[j, 2 * t, :, :] = w.astype(jnp.bfloat16)
            if i == 1 and t == 1:
                w_ref[j, 1, :, :] = w.astype(jnp.bfloat16)


def query_kernel(scale, at_ref, mix_ref, k_ref, q_ref, grad_ref, dqm_ref, dqo_ref, dmix_ref, dq_acc):
    span, width = q_ref.shape
    tile = span // 2
    many = mix_ref.shape[0]

    @pl.when(pl.program_id(0) == 0)
    def _():
        dq_acc[...] = jnp.zeros_like(dq_acc)

    dmix = [jnp.zeros((1, width), jnp.float32) for _ in range(many)]
    for t in (0, 1):
        lo = t * tile
        q_f32 = q_ref[lo:lo + tile, :].astype(jnp.float32)
        dq = 0.0
        for j in range(many):
            qg = dot(grad_ref[j, t], k_ref[lo:lo + 3 * tile, :], TN) * scale
            dq = dq + qg * mix_ref[j]
            dmix[j] = dmix[j] + jnp.sum(qg * q_f32, 0, keepdims=True)
        dq_acc[lo:lo + tile, :] += dq
    for j in range(many):
        for m, block in enumerate(blocks_of(at_ref)):
            dst = pl.ds(pl.multiple_of(block * 128, 128), 128)
            dmix_ref[j, :, dst] = dmix[j][:, m * 128:(m + 1) * 128]

    @pl.when(pl.program_id(0) == pl.num_programs(0) - 1)
    def _():
        dqm_ref[...] = dq_acc[:, :width // 2]
        dqo_ref[...] = dq_acc[:, width // 2:].astype(jnp.bfloat16)


def key_kernel(mix_ref, c_ref, q_ref, grad_ref, w_ref, dk_ref, dv_ref):
    span = q_ref.shape[0]
    tile = span // 2

    @pl.when(pl.program_id(0) == 0)
    def _():
        dk_ref[...] = jnp.zeros_like(dk_ref)

    for j in range(mix_ref.shape[0]):
        cols = slice(j * 128, (j + 1) * 128)
        mq = (q_ref[...].astype(jnp.float32) * mix_ref[j]).astype(jnp.bfloat16)
        dk_ref[...] += dot(grad_ref[j, 1, tile:, :], mq[tile:], NN)
        dk_ref[:tile, :] += dot(grad_ref[j, 0, 2 * tile:, :], mq[:tile], NN)
        dv_ref[tile:, cols] = dot(w_ref[j, 2], c_ref[tile:, cols], NN)
        dv_ref[:tile, cols] = dot(w_ref[j, 1], c_ref[tile:, cols], NN) + dot(w_ref[j, 0], c_ref[:tile, cols], NN)


def next_kernel(scale, at_ref, mix_ref, v_ref, km_ref, ko_ref, cn_ref, qnm_ref, qno_ref, stats_ref,
                dk_ref, dv_ref, dkm_ref, dko_ref, dvo_ref, k_all, q_all, dk_acc):
    span = q_all.shape[0]
    tile = span // 2
    half = km_ref.shape[1]

    @pl.when(pl.program_id(0) == 0)
    def _():
        k_all[:, :half] = km_ref[...]
        k_all[:, half:] = ko_ref[...]
        q_all[:, :half] = qnm_ref[...]
        q_all[:, half:] = qno_ref[...]
        dk_acc[...] = dk_ref[...]

    row = lax.broadcasted_iota(jnp.int32, (tile, tile), 0)
    col = lax.broadcasted_iota(jnp.int32, (tile, tile), 1)
    is_last = at_ref[4] == 1
    seen = (row > col) & jnp.logical_not(is_last)
    for j in range(mix_ref.shape[0]):
        cols = slice(j * 128, (j + 1) * 128)
        dv = [dv_ref[:tile, cols], dv_ref[tile:, cols]]
        for t in (0, 1):
            lo = t * tile
            mq = (q_all[lo:lo + tile, :].astype(jnp.float32) * mix_ref[j]).astype(jnp.bfloat16)
            up = cn_ref[lo:lo + tile, cols]
            lse = stats_ref[j, 0:1, lo:lo + tile]
            delta = stats_ref[j, 1:2, lo:lo + tile]
            s = dot(k_all[lo:, :], mq, NT) * (scale * LOG2E)
            d = dot(v_ref[lo:, cols], up, NT)
            w = jnp.exp2(jnp.where(seen, s[:tile] - lse, NEG))
            if t == 0:
                w = jnp.concatenate([w, jnp.exp2(jnp.where(is_last, NEG, s[tile:] - lse))], 0)
            grad = (w * (d - delta)).astype(jnp.bfloat16)
            add = dot(w.astype(jnp.bfloat16), up, NN)
            if t == 0:
                dv = [dv[0] + add[:tile], dv[1] + add[tile:]]
            else:
                dv[1] = dv[1] + add
            dk_acc[lo:, :] += dot(grad, mq, NN)
        dvo_ref[:tile, cols] = dv[0].astype(jnp.bfloat16)
        dvo_ref[tile:, cols] = dv[1].astype(jnp.bfloat16)

    @pl.when(pl.program_id(0) == pl.num_programs(0) - 1)
    def _():
        dkm_ref[...] = dk_acc[:, :half] * scale
        dko_ref[...] = (dk_acc[:, half:] * scale).astype(jnp.bfloat16)


def load_kernel(v_ref, c_ref, k_ref, q_ref, own0_ref, own1_ref, own2_ref, own3_ref,
                ahead_ref, k_in, q_in, sems):
    core, place = lax.rem(lax.axis_index("head"), 2), lax.rem(lax.axis_index("seq"), GROUP)
    wide = v_ref.shape[1]
    cols = wide // GROUP
    pending = []

    def send(src, dst):
        copy = pltpu.make_async_copy(src, dst, sems.at[len(pending)])
        copy.start()
        pending.append(copy)
        return copy

    shared = [send(k_ref, k_in), send(q_ref, q_in)]
    owns = (own0_ref, own1_ref, own2_ref, own3_ref)
    for e, own in enumerate(owns):
        src = pl.ds(pl.multiple_of(lax.rem(place + e, GROUP) * cols, 128), cols)
        send(v_ref.at[:, src], own.at[:, :cols])
        send(c_ref.at[:, src], own.at[:, cols + 2 * HALF:])
    for copy in shared:
        copy.wait()
    for m in range(2):
        src = pl.ds(pl.multiple_of((2 * m + core) * 128, 128), 128)
        k_block, q_block = k_in[:, src], q_in[:, src]
        ahead_ref[:, m * 128:(m + 1) * 128] = k_block
        for own in owns:
            own[:, cols + m * 128:cols + (m + 1) * 128] = k_block
            own[:, cols + HALF + m * 128:cols + HALF + (m + 1) * 128] = q_block
    for copy in pending[2:]:
        copy.wait()


def split_kernel(at_ref, raw_ref, k_ref, *hops):
    cols = hops[0].shape[1] - HALF
    for e, hop in enumerate(hops):
        src = lax.rem(at_ref[1] + e, GROUP) * cols
        hop[:, :cols] = raw_ref[:, pl.ds(pl.multiple_of(src, 128), cols)]
        hop[:, cols:] = k_ref[...]


def gather_kernel(at_ref, p0_ref, p1_ref, p2_ref, p3_ref, vk_ref, cq_ref, kq_ref):
    half = vk_ref.shape[1]
    for e, ref in enumerate((p0_ref, p1_ref, p2_ref, p3_ref)):
        rows = rows_from(at_ref, e)
        vk_ref[rows, :] = ref[:, :half]
        cq_ref[rows, :half - HALF] = ref[:, half + HALF:]
        cq_ref[rows, half - HALF:] = ref[:, half:half + HALF]
        kq_ref[rows, :] = ref[:, half - HALF:half + HALF]


def collect_kernel(at_ref, mixing_ref, k0_ref, k1_ref, k2_ref, k3_ref, k_ref, mix_ref):
    core, place = at_ref[0], at_ref[1]
    for e, ref in enumerate((k0_ref, k1_ref, k2_ref, k3_ref)):
        k_ref[rows_from(at_ref, e), :] = ref[...]
    for h in range(mix_ref.shape[0]):
        row = mixing_ref[pl.ds(place * mix_ref.shape[0] + h, 1), :]
        blocks = [row[:, i * 128:(i + 1) * 128] for i in range(4)]
        for m, (even, odd) in enumerate(((0, 1), (2, 3), (1, 0), (3, 2))):
            mix_ref[h, :, m * 128:(m + 1) * 128] = jnp.where(core == 0, blocks[even], blocks[odd])


def pack_kernel(at_ref, dv_ref, dk_ref, dk_got_ref, dq_ref, dq_got_ref, *outs):
    cols = dv_ref.shape[1]
    for e, out in enumerate(outs):
        dest = lax.rem(at_ref[1] + e, GROUP)
        rows = pl.ds(pl.multiple_of(dest * 128, 128), 128)
        out[:, :cols] = dv_ref[rows, :]
        dk = dk_ref[rows, :] + dk_got_ref[rows, :].astype(jnp.float32)
        dq = dq_ref[rows, :] + dq_got_ref[rows, :].astype(jnp.float32)
        out[:, cols:cols + HALF] = dk.astype(jnp.bfloat16)
        out[:, cols + HALF:] = dq.astype(jnp.bfloat16)


def sums_kernel(at_ref, *refs):
    parts, (keep_ref, give_ref) = refs[:-2], refs[-2:]
    wide = 0
    y_lo = at_ref[3]
    for m in range(2):
        for ref, which in ((keep_ref, y_lo), (give_ref, 1 - y_lo)):
            src = pl.ds(pl.multiple_of(wide + m * HALF + which * 128, 128), 128)
            total = parts[0][:, src].astype(jnp.float32)
            for part in parts[1:]:
                total = total + part[:, src].astype(jnp.float32)
            ref[:, m * 128:(m + 1) * 128] = total


def values_kernel(at_ref, *refs):
    out = refs[-1]
    cols = out.shape[1] // GROUP
    for e, ref in enumerate(refs[:-1]):
        src = lax.rem(at_ref[1] + GROUP - e, GROUP) * cols
        out[:, pl.ds(pl.multiple_of(src, 128), cols)] = ref[:, :cols]


def last_kernel(keep_ref, got_ref, dk_ref, dq_ref):
    done = (keep_ref[...] + got_ref[...]).astype(jnp.bfloat16)
    dk_ref[...] = done[:, :128]
    dq_ref[...] = done[:, 128:]


def mixing_kernel(at_ref, *refs):
    out = refs[-1]
    rows = refs[0].shape[0]
    for p in range(GROUP):
        block = refs[0][...]
        for e, ref in enumerate(refs[1:-1], 1):
            src = lax.rem(at_ref[1] + GROUP - e, GROUP)
            block = jnp.where(src == p, ref[...], block)
        out[p * rows:(p + 1) * rows, :] = block


SMEM = pl.BlockSpec(memory_space=pltpu.SMEM)
VMEM = pl.BlockSpec(memory_space=pltpu.VMEM)
ANY = pl.BlockSpec(memory_space=pl.ANY)
F32, B16 = jnp.float32, jnp.bfloat16


def call(body, grid, ins, outs, scratch, args, micros, vmem=40):
    return pl.pallas_call(
        body,
        grid=grid,
        in_specs=ins,
        out_specs=[spec for spec, _, _ in outs],
        out_shape=[jax.ShapeDtypeStruct(shape, kind) for _, shape, kind in outs],
        scratch_shapes=scratch,
        compiler_params=pltpu.CompilerParams(vmem_limit_bytes=vmem * 2**20),
        cost_estimate=pl.CostEstimate(
            flops=int(micros * 1e9), bytes_accessed=1_000_000, transcendentals=0),
    )(*args)


def fixed(shape, *at):
    return pl.BlockSpec(shape, lambda h: at or (0,) * len(shape))


def by_head(rows):
    return pl.BlockSpec((rows, 128 * HEADS_AT_ONCE), lambda h: (0, h))


def head_first(*shape):
    return pl.BlockSpec((HEADS_AT_ONCE,) + shape, lambda h: (h,) + (0,) * len(shape))


def per_device(q_shared, k_shared, mixing, values, cotangent):
    tok, width = q_shared.shape
    peers = lax.axis_size("seq")
    scale = 1.0 / math.sqrt(width)
    me = lax.axis_index("seq")
    head_at = lax.axis_index("head")
    heads = mixing.shape[0] // GROUP
    n_v = heads * 128
    span = GROUP * tok
    at = jnp.stack([lax.rem(head_at, 2), lax.rem(me, GROUP), lax.div(me, GROUP), lax.div(head_at, 2),
                    (me >= peers - GROUP).astype(jnp.int32)])

    def to_group(x, by):
        pairs = [(i, (i + GROUP * by) % peers) for i in range(peers)]
        return lax.ppermute(x, "seq", pairs)

    def turn(x, by):
        pairs = [(i, i - i % GROUP + (i + by) % GROUP) for i in range(peers)]
        return lax.ppermute(x, "seq", pairs)

    def turns(parts):
        return [parts[0]] + [turn(part, e) for e, part in enumerate(parts) if e]

    def core_swap(x):
        return lax.ppermute(x, "head", [(0, 1), (1, 0), (2, 3), (3, 2)])

    whole = lambda x: fixed(x.shape)
    wide = n_v + HALF
    ahead_v = to_group(values, 1)
    *own, ahead = call(
        load_kernel, (), [ANY] * 4,
        [(VMEM, (tok, 2 * wide), B16)] * GROUP + [(VMEM, (tok, HALF), B16)],
        [pltpu.VMEM((tok, width), B16)] * 2 + [pltpu.SemaphoreType.DMA((10,))],
        (values, cotangent, k_shared, q_shared), 3, vmem=56)
    ahead = to_group(ahead, 1)
    own = turns(own)
    before = call(split_kernel, (1,), [SMEM, whole(ahead_v), whole(ahead)],
                  [(fixed((tok, wide)), (tok, wide), B16)] * GROUP, [], (at, ahead_v, ahead), 1)
    before = turns(before)
    vk, cq, kq = call(
        gather_kernel, (1,), [SMEM] + [whole(own[0])] * GROUP,
        [(fixed((span, wide)), (span, wide), B16)] * 2
        + [(fixed((span, 2 * HALF)), (span, 2 * HALF), B16)], [], (at, *own), 1)
    cq_next = to_group(cq, -1)
    kq_other = core_swap(kq)
    kp, mix = call(
        collect_kernel, (1,),
        [SMEM, fixed((GROUP * heads, width))] + [fixed((tok, HALF), 0, 2)] * GROUP,
        [(fixed((span, HALF)), (span, HALF), B16),
         (fixed((heads, 1, width)), (heads, 1, width), F32)],
        [], (at, mixing, *before), 1)
    kp_other = core_swap(kp)

    stats, grad, w, k_all, q_all = call(
        functools.partial(scores_kernel, scale), (heads // HEADS_AT_ONCE,),
        [SMEM, head_first(1, width), by_head(span), fixed((span, HALF), 0, 2), by_head(span),
         fixed((span, HALF), 0, n_v // HALF), fixed((span, HALF), 0, 0), fixed((span, HALF), 0, 1)]
        + [by_head(tok)] * GROUP + [fixed((span, HALF))] * 2,
        [(head_first(2, span), (heads, 2, span), F32),
         (head_first(2, 768, 256), (heads, 2, 768, 256), B16),
         (head_first(3, 256, 256), (heads, 3, 256, 256), B16),
         (fixed((2 * span, width)), (2 * span, width), B16),
         (fixed((span, width)), (span, width), B16)],
        [pltpu.VMEM((2 * span, 128 * HEADS_AT_ONCE), B16)],
        (at, mix, vk, vk, cq, cq, kq_other, kq_other, *before, kp, kp_other), 2.5)
    next_stats = to_group(stats, -1)
    dq_mine, dq_other, dmix = call(
        functools.partial(query_kernel, scale), (heads // HEADS_AT_ONCE,),
        [SMEM, head_first(1, width), fixed((2 * span, width)), fixed((span, width)),
         head_first(2, 768, 256)],
        [(fixed((span, HALF)), (span, HALF), F32), (fixed((span, HALF)), (span, HALF), B16),
         (head_first(1, width), (heads, 1, width), F32)],
        [pltpu.VMEM((span, width), F32)],
        (at, mix, k_all, q_all, grad), 0.3)

    def from_peer(x, by):
        return lax.ppermute(x, "seq", [(i, i ^ by) for i in range(peers)])

    def exchange(x, a, b):
        return (x + from_peer(x, a)) + (from_peer(x, b) + from_peer(x, a ^ b))

    dk, dv = call(
        key_kernel, (heads // HEADS_AT_ONCE,),
        [head_first(1, width), by_head(span), fixed((span, width)),
         head_first(2, 768, 256), head_first(3, 256, 256)],
        [(fixed((span, width)), (span, width), F32), (by_head(span), (span, n_v), F32)],
        [], (mix, cq, q_all, grad, w), 0.3)
    cq_next, next_stats, dk, dq_mine = lax.optimization_barrier((cq_next, next_stats, dk, dq_mine))
    q_next_other = core_swap(cq_next[:, n_v:])
    dk_mine, dk_other, dv = call(
        functools.partial(next_kernel, scale), (heads // HEADS_AT_ONCE,),
        [SMEM, head_first(1, width), by_head(span), fixed((span, HALF), 0, 2),
         fixed((span, HALF), 0, 0), by_head(span), fixed((span, HALF), 0, n_v // HALF),
         fixed((span, HALF)), head_first(2, span), fixed((span, width)), by_head(span)],
        [(fixed((span, HALF)), (span, HALF), F32), (fixed((span, HALF)), (span, HALF), B16),
         (by_head(span), (span, n_v), B16)],
        [pltpu.VMEM((span, width), B16), pltpu.VMEM((span, width), B16),
         pltpu.VMEM((span, width), F32)],
        (at, mix, vk, vk, kq_other, cq_next, cq_next, q_next_other, next_stats, dk, dv), 6)
    dk_other, dmix = lax.optimization_barrier((dk_other, dmix))
    dmix = exchange(dmix.reshape(heads, width), GROUP, 8 * GROUP)

    dk_got, dq_got = core_swap(dk_other), core_swap(dq_other)
    back = call(
        pack_kernel, (1,), [SMEM, whole(dv), whole(dk_mine), whole(dk_got), whole(dq_mine), whole(dq_got)],
        [(fixed((tok, n_v + 2 * HALF)), (tok, n_v + 2 * HALF), B16)] * GROUP, [],
        (at, dv, dk_mine, dk_got, dq_mine, dq_got), 1)
    back = turns(back)
    keep, give = call(sums_kernel, (1,), [SMEM] + [fixed((tok, 2 * HALF), 0, n_v // (2 * HALF))] * GROUP,
                      [(fixed((tok, HALF)), (tok, HALF), F32)] * 2, [], (at, *back), 1)
    dmix = exchange(dmix, 2 * GROUP, 4 * GROUP)
    got = lax.ppermute(give, "head", [(0, 2), (1, 3), (2, 0), (3, 1)])
    (d_values,) = call(values_kernel, (1,), [SMEM] + [fixed((tok, n_v))] * GROUP,
                       [(fixed((tok, GROUP * n_v)), (tok, GROUP * n_v), B16)], [], (at, *back), 1)
    d_key, d_query = call(last_kernel, (1,), [whole(keep)] * 2,
                          [(fixed((tok, 128)), (tok, 128), B16)] * 2, [], (keep, got), 1)

    dmix = turns([dmix] * GROUP)
    (d_mixing,) = call(mixing_kernel, (1,), [SMEM] + [whole(dmix[0])] * GROUP,
                       [(fixed((GROUP * heads, width)), (GROUP * heads, width), F32)], [], (at, *dmix), 1)
    return d_query, d_key, d_values, d_mixing


def solution(mesh):
    placed = (P("seq", None), P("seq", None), P("head", None), P("seq", "head"), P("seq", "head"))
    return jax.shard_map(
        per_device,
        mesh=mesh,
        in_specs=placed,
        out_specs=(P("seq", "head"), P("seq", "head"), P("seq", "head"), P("head", None)),
        check_vma=False,
    )
```
